32 devices in a mesh: row: 8 (over y, x, core), col: 4 (over z).
Axes of the slice: x: 2, y: 2, z: 4, core: 2. Of those that a mesh axis runs over, the one named last changes fastest.
Arguments:
- pair_activation: bfloat16 [1024, 1024, 128], P('row', 'col'), may hold values from -80 to 80
- target_distance_bins: int32 [1024, 1024], P('row', 'col'), may hold values from 0 to 63, as said below
- distogram_weight: bfloat16 [128, 64], replicated, may hold values from -2 to 2
- distogram_bias: float32 [64], replicated, may hold values from -0.25 to 0.25
- outer_pair_weight: bfloat16 [1024, 128], replicated, may hold values from -0.1875 to 0.1875
- stored_lhs_operand: bfloat16 [64, 32, 1024], P('row', None, 'col'), may hold values from -6 to 6
- stored_rhs_operand: bfloat16 [64, 32, 1024], P('row', None, 'col'), may hold values from -6 to 6
- left_projection_weight: bfloat16 [64, 32], replicated, may hold values from -0.75 to 0.75
- right_projection_weight: bfloat16 [64, 32], replicated, may hold values from -0.75 to 0.75
- outer_mean_norm_gain: float32 [64], replicated, may hold values from 0.25 to 1.75
- transition_norm_gain: float32 [64], replicated, may hold values from 0.25 to 1.75
- gate_weight: bfloat16 [64, 256], replicated, may hold values from -0.75 to 0.75
- up_weight: bfloat16 [64, 256], replicated, may hold values from -0.75 to 0.75
- down_weight: bfloat16 [256, 64], replicated, may hold values from -0.375 to 0.375
- side_stack_entry: bfloat16 [64, 64, 1024], P(('row', 'col')), may hold values from -6 to 6
- arriving_stack_derivative: bfloat16 [64, 64, 1024], P(('row', 'col')), may hold values from -4 to 4
Outputs:
- pair_activation_gradient: bfloat16 [1024, 1024, 128], P('row', 'col')
- alignment_gradient: bfloat16 [64, 64, 1024], P(('row', 'col'))
The draws below stay inside these ranges and needn't reach their ends.
Inputs may be any that keep to these rules, and one draw needn't show every extreme that they name: target_distance_bins[i, j] equals target_distance_bins[j, i].
All inputs are finite; a program needn't handle non-finite values.
Results may differ from the reference program's by a relative error of at most 0.0098.
Values may be sent and summed in bfloat16 or wider, within the bound.
No kernel may reach another device: no remote copies, remote signals or barrier semaphores. Data moves between devices by JAX's collectives and lax.ppermute only.
A program may use at most 64 MiB of HBM per device.

```python
import jax
import jax.numpy as jnp
from jax import lax

PAIR = 128
SIDE_FEATURE_LEN = 64
COMPONENT_WIDTH = 32
BINS = 64
HID = 256
SPAN_POSITIONS = 1024
OUTER = 1024
ALIGNED_CHAINS = 64


def distance_matrix(key):
    gaussian = jax.random.truncated_normal(jax.random.fold_in(key, 11), -4.0, 4.0, (PAIR, BINS), jnp.float32)
    return gaussian * (2.5 / PAIR ** 0.5)


def mirrored_ints(key, salt_value, upper_bound):
    raw_ints = jax.random.randint(jax.random.fold_in(key, salt_value), (SPAN_POSITIONS, SPAN_POSITIONS), 0, upper_bound)
    return raw_ints + raw_ints.T


def draw_distogram_weight(key, part):
    return distance_matrix(key).astype(jnp.bfloat16)


def draw_target_distance_bins(key, part):
    return (mirrored_ints(key, 21, BINS) % BINS).astype(jnp.int32)


def draw_pair_activation(key, part):
    gaussian = jax.random.truncated_normal(jax.random.fold_in(key, 3), -6.0, 6.0, (SPAN_POSITIONS, SPAN_POSITIONS, PAIR), jnp.float32)
    return gaussian.astype(jnp.bfloat16)


def steps_of(own_key, shape, shards, smallest, top_value):
    gain, own = 1.0, jax.random.fold_in(own_key, 6)
    for dim, shards_of in shards:
        draws = jnp.exp(jax.random.uniform(jax.random.fold_in(own, dim), (shards_of,), jnp.float32, smallest / len(shards), top_value / len(shards)))
        gain = gain * jnp.repeat(draws, shape[dim] // shards_of).reshape([-1 if axis == dim else 1 for axis in range(len(shape))])
    return gain


def bell_draw(stream_key, dims, spread, reach, cuts=(), kind=jnp.bfloat16):
    entries = spread * jax.random.normal(stream_key, dims, jnp.float32)
    if cuts:
        entries = entries * steps_of(stream_key, dims, cuts, -0.22, 0.18)
    return jnp.clip(entries, -reach, reach).astype(kind)


def setup_inputs(seed: int = 0) -> dict:
    key_list = jax.random.split(jax.random.key(seed), 17)
    pair_activation = draw_pair_activation(jax.random.fold_in(key_list[16], 71), 0)
    target_distance_bins = draw_target_distance_bins(jax.random.fold_in(key_list[16], 71), 0)
    distogram_weight = draw_distogram_weight(jax.random.fold_in(key_list[16], 71), 0)
    distogram_bias = jnp.clip(jax.random.uniform(key_list[3], (BINS,), jnp.float32, -0.25, 0.25), -0.25, 0.25)
    outer_pair_weight = bell_draw(key_list[4], (OUTER, PAIR), OUTER ** -0.5, 0.1875)
    stored_lhs_operand = bell_draw(key_list[5], (ALIGNED_CHAINS, COMPONENT_WIDTH, SPAN_POSITIONS), 1.0, 6.0, ((0, 8), (2, 4)))
    stored_rhs_operand = bell_draw(key_list[6], (ALIGNED_CHAINS, COMPONENT_WIDTH, SPAN_POSITIONS), 1.0, 6.0, ((0, 8), (2, 4)))
    left_projection_weight = bell_draw(key_list[7], (SIDE_FEATURE_LEN, COMPONENT_WIDTH), SIDE_FEATURE_LEN ** -0.5, 0.75)
    right_projection_weight = bell_draw(key_list[8], (SIDE_FEATURE_LEN, COMPONENT_WIDTH), SIDE_FEATURE_LEN ** -0.5, 0.75)
    outer_mean_norm_gain = jnp.clip(1.0 + 0.15 * jax.random.normal(key_list[9], (SIDE_FEATURE_LEN,), jnp.float32), 0.25, 1.75)
    transition_norm_gain = jnp.clip(1.0 + 0.15 * jax.random.normal(key_list[10], (SIDE_FEATURE_LEN,), jnp.float32), 0.25, 1.75)
    gate_weight = bell_draw(key_list[11], (SIDE_FEATURE_LEN, HID), SIDE_FEATURE_LEN ** -0.5, 0.75)
    up_weight = bell_draw(key_list[12], (SIDE_FEATURE_LEN, HID), SIDE_FEATURE_LEN ** -0.5, 0.75)
    down_weight = bell_draw(key_list[13], (HID, SIDE_FEATURE_LEN), HID ** -0.5, 0.375)
    side_stack_entry = bell_draw(key_list[14], (ALIGNED_CHAINS, SIDE_FEATURE_LEN, SPAN_POSITIONS), 1.0, 6.0, ((0, 32),))
    arriving_stack_derivative = bell_draw(key_list[15], (ALIGNED_CHAINS, SIDE_FEATURE_LEN, SPAN_POSITIONS), 0.25, 4.0, ((0, 32),))
    return {"pair_activation": pair_activation, "target_distance_bins": target_distance_bins, "distogram_weight": distogram_weight, "distogram_bias": distogram_bias, "outer_pair_weight": outer_pair_weight, "stored_lhs_operand": stored_lhs_operand, "stored_rhs_operand": stored_rhs_operand, "left_projection_weight": left_projection_weight, "right_projection_weight": right_projection_weight, "outer_mean_norm_gain": outer_mean_norm_gain, "transition_norm_gain": transition_norm_gain, "gate_weight": gate_weight, "up_weight": up_weight, "down_weight": down_weight, "side_stack_entry": side_stack_entry, "arriving_stack_derivative": arriving_stack_derivative}


def rounded(tensor):
    return lax.optimization_barrier(tensor.astype(jnp.bfloat16)).astype(jnp.float32)

def apply_layer_norm(features):
    centered = features - lax.optimization_barrier(jnp.mean(features, axis=1, keepdims=True))
    scale_inv = lax.rsqrt(lax.optimization_barrier(jnp.mean(centered * centered, axis=1, keepdims=True)) + 1e-05)
    return (centered * scale_inv, scale_inv)

def norm_backward_step(incoming, normed_field, scale_inv):
    first_mean = lax.optimization_barrier(jnp.mean(incoming, axis=1, keepdims=True))
    second_mean = lax.optimization_barrier(jnp.mean(incoming * normed_field, axis=1, keepdims=True))
    return scale_inv * (incoming - first_mean - normed_field * second_mean)

def reference(pair_activation, target_distance_bins, distogram_weight, distogram_bias, outer_pair_weight, stored_lhs_operand, stored_rhs_operand, left_projection_weight, right_projection_weight, outer_mean_norm_gain, transition_norm_gain, gate_weight, up_weight, down_weight, side_stack_entry, arriving_stack_derivative):
    dist_full = distogram_weight.astype(jnp.float32)
    logits = jnp.einsum('ijp,pb->bij', pair_activation.astype(jnp.float32), dist_full) + distogram_bias[:, None, None]
    logits = rounded(logits)
    symmetric = logits + jnp.swapaxes(logits, 1, 2)
    probability = jax.nn.softmax(symmetric, axis=0)
    bin_levels = jnp.arange(BINS, dtype=jnp.int32)[:, None, None]
    one_hot = (target_distance_bins[None, :, :] == bin_levels).astype(jnp.float32)
    logit_grad = rounded(2.0 * (probability - one_hot))
    pair_activation_gradient = jnp.einsum('bij,pb->ijp', logit_grad, dist_full).astype(jnp.bfloat16)
    outer_full = outer_pair_weight.astype(jnp.float32)
    left_full = stored_lhs_operand.astype(jnp.float32)
    rhs_complete = stored_rhs_operand.astype(jnp.float32)
    block_rows = 32
    tile_number = SPAN_POSITIONS // block_rows

    def single_tile(right_sum, block_index):
        row_start = block_index * block_rows
        grad_rows = lax.dynamic_slice_in_dim(pair_activation_gradient, row_start, block_rows, 0).astype(jnp.float32)
        tensor_product_derivative = rounded(jnp.einsum('ijp,kp->ijk', grad_rows, outer_full))
        tensor_product_derivative = tensor_product_derivative.reshape(block_rows, SPAN_POSITIONS, COMPONENT_WIDTH, COMPONENT_WIDTH)
        lhs_lines = lax.dynamic_slice_in_dim(left_full, row_start, block_rows, 2)
        lhs_portion = jnp.einsum('tdpa,wad->wpt', tensor_product_derivative, rhs_complete) / ALIGNED_CHAINS
        rhs_portion = jnp.einsum('doyw,vyd->vwo', tensor_product_derivative, lhs_lines) / ALIGNED_CHAINS
        return (right_sum + rhs_portion, lhs_portion)
    rhs_derivative, lhs_tiles = lax.scan(single_tile, jnp.zeros((ALIGNED_CHAINS, COMPONENT_WIDTH, SPAN_POSITIONS), jnp.float32), jnp.arange(tile_number, dtype=jnp.int32))
    lhs_derivative = jnp.transpose(lhs_tiles, (1, 2, 0, 3)).reshape(ALIGNED_CHAINS, COMPONENT_WIDTH, SPAN_POSITIONS)
    norm_input_gradient = jnp.einsum('mc,sci->smi', left_projection_weight.astype(jnp.float32), lhs_derivative, precision=lax.Precision.HIGHEST)
    norm_input_gradient = norm_input_gradient + jnp.einsum('me,sei->smi', right_projection_weight.astype(jnp.float32), rhs_derivative, precision=lax.Precision.HIGHEST)
    norm_input_gradient = rounded(norm_input_gradient)
    alignment_widened = side_stack_entry.astype(jnp.float32)
    first_normed_rows, first_inverse_scale = apply_layer_norm(alignment_widened)
    normed_input = rounded(first_normed_rows * transition_norm_gain[None, :, None])
    gate_value = jnp.einsum('smi,mh->shi', normed_input, gate_weight.astype(jnp.float32))
    upward = jnp.einsum('smi,mh->shi', normed_input, up_weight.astype(jnp.float32))
    hidden_state = rounded(jax.nn.silu(gate_value) * upward)
    alignment_output = alignment_widened + jnp.einsum('ajc,jr->arc', hidden_state, down_weight.astype(jnp.float32))
    second_normed_rows, second_inverse_scale = apply_layer_norm(alignment_output)
    middle_gradient = arriving_stack_derivative.astype(jnp.float32) + norm_backward_step(norm_input_gradient * outer_mean_norm_gain[None, :, None], second_normed_rows, second_inverse_scale)
    mid_half = rounded(middle_gradient)
    hidden_grad = jnp.einsum('smi,hm->shi', mid_half, down_weight.astype(jnp.float32))
    sigmoid_gate = jax.nn.sigmoid(gate_value)
    gate_grad = rounded(hidden_grad * upward * sigmoid_gate * (1.0 + gate_value * (1.0 - sigmoid_gate)))
    up_grad = rounded(hidden_grad * gate_value * sigmoid_gate)
    normed_rows_gradient = jnp.einsum('shi,mh->smi', gate_grad, gate_weight.astype(jnp.float32))
    normed_rows_gradient = normed_rows_gradient + jnp.einsum('shi,mh->smi', up_grad, up_weight.astype(jnp.float32))
    alignment_gradient = middle_gradient + norm_backward_step(normed_rows_gradient * transition_norm_gain[None, :, None], first_normed_rows, first_inverse_scale)
    return (pair_activation_gradient, alignment_gradient.astype(jnp.bfloat16))
```

```python
import functools

import jax
import jax.numpy as jnp
from jax import lax
from jax.experimental import pallas as pl
from jax.experimental.pallas import tpu as pltpu
from jax.sharding import PartitionSpec as P

BF16, F32 = jnp.bfloat16, jnp.float32
VMEM_BYTES = 56 * 1024 * 1024
AXES = ("row", "col")
GROUP = 4


def contract(lhs, rhs, lhs_dim, rhs_dim):
    return lax.dot_general(
        lhs, rhs, (((lhs_dim,), (rhs_dim,)), ((), ())), preferred_element_type=F32
    )


def relay(block, z, blocks):
    if blocks % 4:
        return z, block
    low_block = ((1 - (block & 1)) << 1) | (z & 1)
    low_z = (z & 2) | ((block >> 1) & 1)
    return (z >> 2 << 2) | low_block, (block >> 2 << 2) | low_z


def first_leg(blocks, parts):
    pairs = []
    for block in range(blocks):
        for z in range(blocks):
            to_block, to_z = relay(block, z, blocks)
            for h in range(parts):
                pairs.append(
                    ((block * parts + h) * blocks + z, (to_block * parts + h) * blocks + to_z)
                )
    return pairs


def second_leg(blocks, parts, shift):
    pairs = []
    for block in range(blocks):
        for z in range(blocks):
            via_block, via_z = relay(block, z, blocks)
            for h in range(parts):
                pairs.append(
                    (
                        (via_block * parts + h) * blocks + via_z,
                        (z * parts + (h + shift) % parts) * blocks + block,
                    )
                )
    return pairs


def mirror_logits_kernel(part_ref, pair_ref, weight_ref, bias_ref, out_ref, widened):
    own_rows, step_cols, width = pair_ref.shape
    widened[...] = pair_ref[...].astype(F32).reshape(own_rows * step_cols, width)
    weight = weight_ref[...]
    bias = bias_ref[...]
    for j in range(step_cols):
        column = widened[pl.ds(j, own_rows, stride=step_cols), :].astype(BF16)
        out_ref[j] = (contract(weight, column, 1, 1) + bias).astype(BF16)


def mirror_logits(part, pair_activation, weight_t, bias, chunk, chunks, shift, parts):
    rows, cols, width = pair_activation.shape
    bins = weight_t.shape[0]
    chunk_rows = rows // chunks
    step = min(16, chunk_rows)
    steps = chunk_rows // step

    def block(s, part_ref):
        half = lax.rem(part_ref[0] + shift, parts)
        return (0, half * (rows // step) + chunk * steps + s, 0)

    return pl.pallas_call(
        mirror_logits_kernel,
        grid_spec=pltpu.PrefetchScalarGridSpec(
            num_scalar_prefetch=1,
            grid=(steps,),
            in_specs=[
                pl.BlockSpec((rows, step, width), block),
                pl.BlockSpec((bins, width), lambda s, p: (0, 0)),
                pl.BlockSpec((bins, 1), lambda s, p: (0, 0)),
            ],
            out_specs=pl.BlockSpec((step, bins, rows), lambda s, p: (s, 0, 0)),
            scratch_shapes=[pltpu.VMEM((rows * step, width), F32)],
        ),
        out_shape=jax.ShapeDtypeStruct((chunk_rows, bins, rows), BF16),
        compiler_params=pltpu.CompilerParams(vmem_limit_bytes=VMEM_BYTES),
        cost_estimate=pl.CostEstimate(
            flops=2 * chunk_rows * rows * bins * width * 4,
            bytes_accessed=chunk_rows * rows * (width + bins) * 2,
            transcendentals=0,
        ),
        name="mirror_logits",
    )(part, pair_activation, weight_t, bias)


def pair_kernel(
    parts, part_ref, pair_ref, *refs
):
    received = refs[:parts]
    target_ref, weight_t_ref, weight_ref, bias_ref, factor_ref, mix_ref = refs[parts : parts + 6]
    grad_ref, norm_ref, slopes, mixed, total = refs[-5:]
    step = pl.program_id(0)
    steps = pl.num_programs(0)
    chunk_rows, cols, _ = pair_ref.shape
    bins = weight_t_ref.shape[0]
    own_rows = cols // parts
    groups = chunk_rows // GROUP
    seqs = norm_ref.shape[0]
    lanes = GROUP * norm_ref.shape[1] // chunk_rows
    xs = factor_ref.shape[0] // seqs

    @pl.when(step == 0)
    def _():
        h = part_ref[0]
        weight_t = weight_t_ref[...]
        weight = weight_ref[...]
        bias = bias_ref[...]
        levels = lax.broadcasted_iota(jnp.int32, (bins, cols), 0)
        for g in range(groups):
            for r in range(GROUP):
                i = g * GROUP + r
                own = (contract(weight_t, pair_ref[i], 1, 1) + bias).astype(BF16).astype(F32)
                halves = []
                for u in range(parts):
                    half = received[0][i]
                    for shift in range(1, parts):
                        half = jnp.where(lax.rem(h + parts - u, parts) == shift, received[shift][i], half)
                    halves.append(half)
                symmetric = own + jnp.concatenate(halves, axis=1).astype(F32)
                top = jnp.max(symmetric, axis=0, keepdims=True)
                raised = jnp.exp(symmetric - top)
                scale = 2.0 / jnp.sum(raised, axis=0, keepdims=True)
                hit = jnp.where(levels == target_ref[i : i + 1, :], 2.0, 0.0)
                slope = (raised * scale - hit).astype(BF16)
                slopes[g, r * bins : (r + 1) * bins, :] = slope
                grad_ref[i] = contract(slope, weight, 0, 1).astype(BF16)
        total[...] = jnp.zeros_like(total)

    factor = factor_ref[...]
    for g in range(groups):
        spread = contract(factor, slopes[g], 1, 1).astype(BF16)
        for x in range(xs):
            mixed[g * seqs : (g + 1) * seqs, x * GROUP * bins : (x + 1) * GROUP * bins] = (
                spread[x * seqs : (x + 1) * seqs, :]
            )
    total[...] += contract(mixed[...], mix_ref[...], 1, 0)

    @pl.when(step == steps - 1)
    def _():
        for g in range(groups):
            norm_ref[:, g * lanes : (g + 1) * lanes] = (
                total[g * seqs : (g + 1) * seqs, :].astype(BF16)
            )


def pair_step(
    part, pair_activation, received, targets, weight_t, weight, bias, factors, mix, grad, chunk,
    chunks, seqs, features, tile,
):
    rows, cols, width = pair_activation.shape
    bins = weight_t.shape[0]
    parts = len(received)
    chunk_rows = rows // chunks
    groups = chunk_rows // GROUP
    xs = factors.shape[0] // seqs
    steps = xs // tile
    const2 = lambda s, p: (0, 0)
    const3 = lambda s, p: (0, 0, 0)
    return pl.pallas_call(
        functools.partial(pair_kernel, parts),
        grid_spec=pltpu.PrefetchScalarGridSpec(
            num_scalar_prefetch=1,
            grid=(steps,),
            in_specs=[pl.BlockSpec((chunk_rows, cols, width), lambda s, p: (chunk, 0, 0))]
            + [pl.BlockSpec((chunk_rows, bins, cols // parts), const3)] * parts
            + [
                pl.BlockSpec((chunk_rows, cols), lambda s, p: (chunk, 0)),
                pl.BlockSpec((bins, width), const2),
                pl.BlockSpec((width, bins), const2),
                pl.BlockSpec((bins, 1), const2),
                pl.BlockSpec((tile * seqs, cols), lambda s, p: (s, 0)),
                pl.BlockSpec((tile * GROUP * bins, GROUP * features), lambda s, p: (s, 0)),
            ]
            + [pl.BlockSpec(memory_space=pl.ANY)] * len(grad),
            out_specs=[
                pl.BlockSpec((chunk_rows, cols, width), lambda s, p: (chunk, 0, 0)),
                pl.BlockSpec((seqs, chunk_rows * features), const2),
            ],
            scratch_shapes=[
                pltpu.VMEM((groups, GROUP * bins, cols), BF16),
                pltpu.VMEM((groups * seqs, tile * GROUP * bins), BF16),
                pltpu.VMEM((groups * seqs, GROUP * features), F32),
            ],
        ),
        out_shape=[
            jax.ShapeDtypeStruct(pair_activation.shape, BF16),
            jax.ShapeDtypeStruct((seqs, chunk_rows * features), BF16),
        ],
        input_output_aliases={parts + 8: 0} if grad else {},
        compiler_params=pltpu.CompilerParams(vmem_limit_bytes=VMEM_BYTES),
        cost_estimate=pl.CostEstimate(
            flops=4 * xs * seqs * cols * chunk_rows * bins,
            bytes_accessed=chunk_rows * cols * width * 6,
            transcendentals=chunk_rows * cols * bins,
        ),
        name="pair_step",
    )(part, pair_activation, *received, targets, weight_t, weight, bias, factors, mix, *grad)


def norm_forward(features):
    centered = features - jnp.mean(features, axis=0, keepdims=True)
    scale_inv = lax.rsqrt(jnp.mean(centered * centered, axis=0, keepdims=True) + 1e-05)
    return centered * scale_inv, scale_inv


def norm_backward(incoming, normed, scale_inv):
    first_mean = jnp.mean(incoming, axis=0, keepdims=True)
    second_mean = jnp.mean(incoming * normed, axis=0, keepdims=True)
    return scale_inv * (incoming - first_mean - normed * second_mean)


def transition_kernel(
    entry_ref, arriving_ref, incoming_ref, mean_gain_ref, gain_ref, gate_up_t_ref, gate_up_ref,
    down_ref, down_t_ref, out_ref,
):
    hidden = down_ref.shape[0]
    entry = entry_ref[0].astype(F32)
    normed, scale_inv = norm_forward(entry)
    gain = gain_ref[...]
    normed_input = (normed * gain).astype(BF16)
    both = contract(gate_up_t_ref[...], normed_input, 1, 0)
    gate, up = both[:hidden], both[hidden:]
    sig = jax.nn.sigmoid(gate)
    silu = gate * sig
    msa_out = entry + contract(down_t_ref[...], (silu * up).astype(BF16), 1, 0)
    second_normed, second_scale = norm_forward(msa_out)
    middle = arriving_ref[0].astype(F32) + norm_backward(
        incoming_ref[0].astype(F32) * mean_gain_ref[...], second_normed, second_scale
    )
    hidden_grad = contract(down_ref[...], middle.astype(BF16), 1, 0)
    gate_grad = (hidden_grad * up * sig * (1.0 + gate * (1.0 - sig))).astype(BF16)
    up_grad = (hidden_grad * silu).astype(BF16)
    normed_grad = contract(gate_up_ref[...], jnp.concatenate([gate_grad, up_grad], axis=0), 1, 0)
    out = middle + norm_backward(normed_grad * gain, normed, scale_inv)
    out_ref[0] = out.astype(BF16)


def transition(entry, arriving, incoming, mean_gain, gain, gate_weight, up_weight, down_weight):
    seqs, features, positions = entry.shape
    hidden = down_weight.shape[0]
    gate_up = jnp.concatenate([gate_weight, up_weight], axis=1)
    step = min(512, positions)
    field = pl.BlockSpec((1, features, step), lambda s, i: (s, 0, i))
    whole = lambda shape: pl.BlockSpec(shape, lambda s, i: (0, 0))
    return pl.pallas_call(
        transition_kernel,
        grid=(seqs, positions // step),
        in_specs=[field, field, field, whole((features, 1)), whole((features, 1)),
                  whole((2 * hidden, features)), whole((features, 2 * hidden)),
                  whole((hidden, features)), whole((features, hidden))],
        out_specs=field,
        out_shape=jax.ShapeDtypeStruct(entry.shape, BF16),
        compiler_params=pltpu.CompilerParams(vmem_limit_bytes=VMEM_BYTES),
        name="transition",
    )(entry, arriving, incoming, mean_gain[:, None], gain[:, None], gate_up.T, gate_up,
      down_weight, down_weight.T)


def per_device(
    pair_activation,
    target_distance_bins,
    distogram_weight,
    distogram_bias,
    outer_pair_weight,
    stored_lhs_operand,
    stored_rhs_operand,
    left_projection_weight,
    right_projection_weight,
    outer_mean_norm_gain,
    transition_norm_gain,
    gate_weight,
    up_weight,
    down_weight,
    side_stack_entry,
    arriving_stack_derivative,
):
    rows, cols, _ = pair_activation.shape
    width, bins = distogram_weight.shape
    factor_width = stored_lhs_operand.shape[1]
    features = left_projection_weight.shape[0]
    row_devices = lax.axis_size("row")
    col_devices = lax.axis_size("col")
    parts = row_devices // col_devices
    seqs = stored_lhs_operand.shape[0] * row_devices
    chunks = max(1, min(4, rows // 16))
    chunk_rows = rows // chunks
    part = (lax.axis_index("row") % parts).astype(jnp.int32)[None]
    weight_t = distogram_weight.T
    bias = distogram_bias[:, None]

    leg_pairs = first_leg(col_devices, parts)
    received = []
    landed = []
    for chunk in range(chunks):
        pieces = [
            mirror_logits(part, pair_activation, weight_t, bias, chunk, chunks, shift, parts)
            for shift in range(parts)
        ]
        if chunk >= 2:
            *pieces, _ = lax.optimization_barrier((*pieces, landed[chunk - 2][0]))
        relayed = [lax.ppermute(piece, AXES, leg_pairs) for piece in pieces]
        landed.append(relayed)
        received.append(
            [
                lax.ppermute(piece, AXES, second_leg(col_devices, parts, shift))
                for shift, piece in enumerate(relayed)
            ]
        )

    left_all = lax.all_gather(stored_lhs_operand, "row", axis=0, tiled=True)
    right_all = lax.all_gather(stored_rhs_operand, "row", axis=0, tiled=True)
    factors = jnp.concatenate(
        [jnp.swapaxes(right_all, 0, 1), jnp.swapaxes(left_all, 0, 1)], axis=0
    ).reshape(2 * factor_width * seqs, cols)

    outer_weight = outer_pair_weight.astype(F32).reshape(factor_width, factor_width, width)
    by_bin = jnp.einsum(
        "pb,cep->bce", distogram_weight.astype(F32), outer_weight, precision=lax.Precision.HIGHEST
    )
    mix_right = jnp.einsum(
        "mc,bce->ebm", left_projection_weight.astype(F32), by_bin, precision=lax.Precision.HIGHEST
    )
    mix_left = jnp.einsum(
        "me,bce->cbm", right_projection_weight.astype(F32), by_bin, precision=lax.Precision.HIGHEST
    )
    mix = (jnp.concatenate([mix_right, mix_left], axis=0) / seqs).astype(BF16)
    same = jnp.eye(GROUP, dtype=BF16)
    mix = (mix[:, None, :, None, :] * same[None, :, None, :, None]).reshape(
        2 * factor_width * GROUP * bins, GROUP * features
    )

    grad = None
    tile = max(1, min(8, 512 // seqs))
    fields = []
    for chunk in range(chunks):
        grad, norm_part = pair_step(
            part, pair_activation, received[chunk], target_distance_bins, weight_t,
            distogram_weight, bias, factors, mix, () if grad is None else (grad,), chunk, chunks,
            seqs, features, tile,
        )
        parts_in = lax.all_to_all(norm_part, AXES, split_axis=0, concat_axis=0, tiled=True)
        fields.append(
            parts_in.reshape(row_devices, col_devices, -1, chunk_rows, features)
            .astype(F32)
            .sum(axis=1)
        )
    incoming = jnp.stack(fields).astype(BF16).transpose(2, 4, 1, 0, 3)
    incoming = incoming.reshape(side_stack_entry.shape)
    alignment_gradient = transition(
        side_stack_entry, arriving_stack_derivative, incoming, outer_mean_norm_gain,
        transition_norm_gain, gate_weight, up_weight, down_weight,
    )
    return grad, alignment_gradient


def solution(mesh):
    return jax.shard_map(
        per_device,
        mesh=mesh,
        in_specs=(
            P("row", "col", None),
            P("row", "col"),
            P(),
            P(),
            P(),
            P("row", None, "col"),
            P("row", None, "col"),
            P(),
            P(),
            P(),
            P(),
            P(),
            P(),
            P(),
            P(AXES, None, None),
            P(AXES, None, None),
        ),
        out_specs=(P("row", "col", None), P(AXES, None, None)),
        check_vma=False,
    )
```

```python
import functools

import jax
import jax.numpy as jnp
from jax import lax
from jax.experimental import pallas as pl
from jax.experimental.pallas import tpu as pltpu
from jax.sharding import PartitionSpec as P

BF16, F32 = jnp.bfloat16, jnp.float32
VMEM_BYTES = 56 * 1024 * 1024
AXES = ("row", "col")
GROUP = 4


def contract(lhs, rhs, lhs_dim, rhs_dim):
    return lax.dot_general(
        lhs, rhs, (((lhs_dim,), (rhs_dim,)), ((), ())), preferred_element_type=F32
    )


def relay(block, z, blocks):
    if blocks % 4:
        return z, block
    low_block = ((1 - (block & 1)) << 1) | (z & 1)
    low_z = (z & 2) | ((block >> 1) & 1)
    return (z >> 2 << 2) | low_block, (block >> 2 << 2) | low_z


def first_leg(blocks, parts):
    pairs = []
    for block in range(blocks):
        for z in range(blocks):
            to_block, to_z = relay(block, z, blocks)
            for h in range(parts):
                pairs.append(
                    ((block * parts + h) * blocks + z, (to_block * parts + h) * blocks + to_z)
                )
    return pairs


def second_leg(blocks, parts, shift):
    pairs = []
    for block in range(blocks):
        for z in range(blocks):
            via_block, via_z = relay(block, z, blocks)
            for h in range(parts):
                pairs.append(
                    (
                        (via_block * parts + h) * blocks + via_z,
                        (z * parts + (h + shift) % parts) * blocks + block,
                    )
                )
    return pairs


def mirror_logits_kernel(part_ref, pair_ref, weight_ref, bias_ref, out_ref, widened):
    own_rows, step_cols, width = pair_ref.shape
    widened[...] = pair_ref[...].astype(F32).reshape(own_rows * step_cols, width)
    weight = weight_ref[...]
    bias = bias_ref[...]
    for j in range(step_cols):
        column = widened[pl.ds(j, own_rows, stride=step_cols), :].astype(BF16)
        out_ref[j] = (contract(weight, column, 1, 1) + bias).astype(BF16)


def mirror_logits(part, pair_activation, weight_t, bias, first_row, chunk_rows, shift, parts):
    rows, cols, width = pair_activation.shape
    bins = weight_t.shape[0]
    step = min(16, chunk_rows)
    steps = chunk_rows // step

    def block(s, part_ref):
        half = lax.rem(part_ref[0] + shift, parts)
        return (0, half * (rows // step) + first_row // step + s, 0)

    return pl.pallas_call(
        mirror_logits_kernel,
        grid_spec=pltpu.PrefetchScalarGridSpec(
            num_scalar_prefetch=1,
            grid=(steps,),
            in_specs=[
                pl.BlockSpec((rows, step, width), block),
                pl.BlockSpec((bins, width), lambda s, p: (0, 0)),
                pl.BlockSpec((bins, 1), lambda s, p: (0, 0)),
            ],
            out_specs=pl.BlockSpec((step, bins, rows), lambda s, p: (s, 0, 0)),
            scratch_shapes=[pltpu.VMEM((rows * step, width), F32)],
        ),
        out_shape=jax.ShapeDtypeStruct((chunk_rows, bins, rows), BF16),
        compiler_params=pltpu.CompilerParams(vmem_limit_bytes=VMEM_BYTES),
        cost_estimate=pl.CostEstimate(
            flops=2 * chunk_rows * rows * bins * width * 4,
            bytes_accessed=chunk_rows * rows * (width + bins) * 2,
            transcendentals=0,
        ),
        name="mirror_logits",
    )(part, pair_activation, weight_t, bias)


def pair_kernel(parts, front, tile, part_ref, pair_ref, *refs):
    received = refs[:parts]
    target_ref, weight_t_ref, weight_wide_ref, bias_ref, factor_hbm, mix_hbm = refs[parts : parts + 6]
    grad_ref, norm_ref, slopes, factors, mix, mix_wide, mixed, total, sems = refs[-9:]
    step = pl.program_id(0)
    step_rows, cols, width = pair_ref.shape
    bins = weight_t_ref.shape[0]
    groups = slopes.shape[0]
    step_groups = step_rows // GROUP
    features = total.shape[0] * total.shape[2] // GROUP
    devices, device_rows, _ = norm_ref.shape
    device_seqs = device_rows // groups
    seqs = devices * device_seqs
    xs = mix.shape[0]
    copies = [
        pltpu.make_async_copy(factor_hbm, factors, sems.at[0]),
        pltpu.make_async_copy(mix_hbm, mix, sems.at[1]),
    ]

    @pl.when(step == 0)
    def _():
        for copy in copies:
            copy.start()
        total[...] = jnp.zeros_like(total)
        mix_wide[...] = jnp.zeros_like(mix_wide)

    @pl.when(step < front)
    def _():
        h = part_ref[0]
        weight_t = weight_t_ref[...]
        bias = bias_ref[...]
        levels = lax.broadcasted_iota(jnp.int32, (bins, cols), 0)
        for g in range(step_groups):
            group = []
            for r in range(GROUP):
                i = g * GROUP + r
                own = (contract(weight_t, pair_ref[i], 1, 1) + bias).astype(BF16).astype(F32)
                halves = []
                for u in range(parts):
                    half = received[0][i]
                    for shift in range(1, parts):
                        half = jnp.where(
                            lax.rem(h + parts - u, parts) == shift, received[shift][i], half
                        )
                    halves.append(half)
                symmetric = own + jnp.concatenate(halves, axis=1).astype(F32)
                top = jnp.max(symmetric, axis=0, keepdims=True)
                raised = jnp.exp(symmetric - top)
                scale = 2.0 / jnp.sum(raised, axis=0, keepdims=True)
                hit = jnp.where(levels == target_ref[i : i + 1, :], 2.0, 0.0)
                group.append((raised * scale - hit).astype(BF16))
            slope = jnp.concatenate(group, axis=0).T
            slopes[step * step_groups + g] = slope
            out = contract(slope, weight_wide_ref[...], 1, 0).astype(BF16)
            for r in range(GROUP):
                grad_ref[g * GROUP + r] = out[:, r * width : (r + 1) * width]

    @pl.when(step == front)
    def _():
        for copy in copies:
            copy.wait()
        half_groups = max(1, min(groups, 256 // seqs))

        def add_tile(t, carry):
            for x in range(tile):
                for r in range(GROUP):
                    rows = pl.ds((x * GROUP + r) * bins, bins)
                    at = r * features
                    mix_wide[rows, at : at + features] = (
                        mix[t * tile + x, :, at % 128 : at % 128 + features]
                    )
            factor = factors[pl.ds(pl.multiple_of(t * tile * seqs, tile * seqs), tile * seqs), :]
            for g in range(groups):
                spread = contract(factor, slopes[g], 1, 0).astype(BF16)
                for x in range(tile):
                    mixed[g * seqs : (g + 1) * seqs, x * GROUP * bins : (x + 1) * GROUP * bins] = (
                        spread[x * seqs : (x + 1) * seqs, :]
                    )
            for g in range(0, groups, half_groups):
                rows = slice(g * seqs, (g + half_groups) * seqs)
                term = contract(mixed[rows, :], mix_wide[...], 1, 0)
                for c in range(total.shape[0]):
                    total[c, rows, :] += term[:, c * 128 : (c + 1) * 128]
            return carry

        lax.fori_loop(0, xs // tile, add_tile, 0)
        for s in range(seqs):
            device, k = divmod(s, device_seqs)
            for c in range(total.shape[0]):
                norm_ref[device, k * groups : (k + 1) * groups, c * 128 : (c + 1) * 128] = (
                    total[c, pl.ds(s, groups, stride=seqs), :].astype(BF16)
                )


def pair_step(
    part, pair_activation, received, targets, weight_t, weight_wide, bias, factors, mix, grad,
    first_row, seqs, devices,
):
    _, cols, width = pair_activation.shape
    bins = weight_t.shape[0]
    features = mix.shape[2] // 2
    parts = len(received)
    chunk_rows = received[0].shape[0]
    step_rows = min(16, chunk_rows)
    groups = chunk_rows // GROUP
    xs = factors.shape[0] // seqs
    tile = max(1, min(8, 512 // seqs))
    front = chunk_rows // step_rows
    near = lambda s: jnp.minimum(s, front - 1)
    there = lambda s: first_row // step_rows + jnp.minimum(s, front - 1)
    const2 = lambda s, p: (0, 0)
    norm_shape = (devices, seqs // devices * groups, GROUP * features)
    return pl.pallas_call(
        functools.partial(pair_kernel, parts, front, tile),
        grid_spec=pltpu.PrefetchScalarGridSpec(
            num_scalar_prefetch=1,
            grid=(front + 1,),
            in_specs=[pl.BlockSpec((step_rows, cols, width), lambda s, p: (there(s), 0, 0))]
            + [pl.BlockSpec((step_rows, bins, cols // parts), lambda s, p: (near(s), 0, 0))] * parts
            + [
                pl.BlockSpec((step_rows, cols), lambda s, p: (there(s), 0)),
                pl.BlockSpec((bins, width), const2),
                pl.BlockSpec((GROUP * bins, GROUP * width), const2),
                pl.BlockSpec((bins, 1), const2),
            ]
            + [pl.BlockSpec(memory_space=pl.ANY)] * (2 + len(grad)),
            out_specs=[
                pl.BlockSpec((step_rows, cols, width), lambda s, p: (there(s), 0, 0)),
                pl.BlockSpec(norm_shape, lambda s, p: (0, 0, 0)),
            ],
            scratch_shapes=[
                pltpu.VMEM((groups, cols, GROUP * bins), BF16),
                pltpu.VMEM(factors.shape, BF16),
                pltpu.VMEM(mix.shape, BF16),
                pltpu.VMEM((tile * GROUP * bins, GROUP * features), BF16),
                pltpu.VMEM((groups * seqs, tile * GROUP * bins), BF16),
                pltpu.VMEM((GROUP * features // 128, groups * seqs, 128), F32),
                pltpu.SemaphoreType.DMA((2,)),
            ],
        ),
        out_shape=[
            jax.ShapeDtypeStruct(pair_activation.shape, BF16),
            jax.ShapeDtypeStruct(norm_shape, BF16),
        ],
        input_output_aliases={parts + 8: 0} if grad else {},
        compiler_params=pltpu.CompilerParams(vmem_limit_bytes=VMEM_BYTES),
        cost_estimate=pl.CostEstimate(
            flops=4 * xs * seqs * cols * chunk_rows * bins,
            bytes_accessed=chunk_rows * cols * width * 6,
            transcendentals=chunk_rows * cols * bins,
        ),
        name="pair_step",
    )(part, pair_activation, *received, targets, weight_t, weight_wide, bias, factors, mix, *grad)


def norm_forward(features):
    centered = features - jnp.mean(features, axis=0, keepdims=True)
    scale_inv = lax.rsqrt(jnp.mean(centered * centered, axis=0, keepdims=True) + 1e-05)
    return centered * scale_inv, scale_inv


def norm_backward(incoming, normed, scale_inv):
    first_mean = jnp.mean(incoming, axis=0, keepdims=True)
    second_mean = jnp.mean(incoming * normed, axis=0, keepdims=True)
    return scale_inv * (incoming - first_mean - normed * second_mean)


def transition_kernel(
    pieces, rows, col_devices, entry_ref, arriving_ref, mean_gain_ref, gain_ref, gate_up_t_ref,
    gate_up_ref, down_ref, down_t_ref, *refs,
):
    arrived, (out_ref, incoming) = refs[:-2], refs[-2:]
    hidden = down_ref.shape[0]
    seqs, features, positions = out_ref.shape
    groups = rows // GROUP
    row = lax.broadcasted_iota(jnp.int32, (groups, rows), 0)
    col = lax.broadcasted_iota(jnp.int32, (groups, rows), 1)
    spread = [jnp.where(col == GROUP * row + r, 1.0, 0.0).astype(BF16) for r in range(GROUP)]

    for s in range(seqs):
        for block in range(positions // rows):
            sums = []
            for which, at, count in pieces:
                at += s * count
                sums.append(
                    sum(
                        arrived[which][block * col_devices + c, at : at + count, :].astype(F32)
                        for c in range(col_devices)
                    )
                )
            field = jnp.concatenate(sums, axis=0).astype(BF16)
            incoming[s, :, block * rows : (block + 1) * rows] = sum(
                contract(field[:, r * features : (r + 1) * features], spread[r], 0, 0)
                for r in range(GROUP)
            )

    gain = gain_ref[...]
    for s in range(seqs):
        entry = entry_ref[s].astype(F32)
        normed, scale_inv = norm_forward(entry)
        normed_input = (normed * gain).astype(BF16)
        both = contract(gate_up_t_ref[...], normed_input, 1, 0)
        gate, up = both[:hidden], both[hidden:]
        sig = jax.nn.sigmoid(gate)
        silu = gate * sig
        msa_out = entry + contract(down_t_ref[...], (silu * up).astype(BF16), 1, 0)
        second_normed, second_scale = norm_forward(msa_out)
        middle = arriving_ref[s].astype(F32) + norm_backward(
            incoming[s] * mean_gain_ref[...], second_normed, second_scale
        )
        hidden_grad = contract(down_ref[...], middle.astype(BF16), 1, 0)
        gate_grad = (hidden_grad * up * sig * (1.0 + gate * (1.0 - sig))).astype(BF16)
        up_grad = (hidden_grad * silu).astype(BF16)
        normed_grad = contract(
            gate_up_ref[...], jnp.concatenate([gate_grad, up_grad], axis=0), 1, 0
        )
        out = middle + norm_backward(normed_grad * gain, normed, scale_inv)
        out_ref[s] = out.astype(BF16)


def transition(
    entry, arriving, arrived, pieces, rows, col_devices, mean_gain, gain, gate_weight, up_weight,
    down_weight,
):
    features = entry.shape[1]
    gate_up = jnp.concatenate([gate_weight, up_weight], axis=1)
    return pl.pallas_call(
        functools.partial(transition_kernel, pieces, rows, col_devices),
        out_shape=jax.ShapeDtypeStruct(entry.shape, BF16),
        scratch_shapes=[pltpu.VMEM(entry.shape, F32)],
        compiler_params=pltpu.CompilerParams(vmem_limit_bytes=VMEM_BYTES),
        name="transition",
    )(entry, arriving, mean_gain[:, None], gain[:, None], gate_up.T, gate_up, down_weight,
      down_weight.T, *arrived)


def chunk_plan(rows):
    sizes = []
    while rows - sum(sizes) > 32:
        sizes.append(32)
    left = rows - sum(sizes)
    sizes += [16, left - 16] if left > 16 else [left]
    return [(sum(sizes[:n]), size) for n, size in enumerate(sizes)]


def per_device(
    pair_activation,
    target_distance_bins,
    distogram_weight,
    distogram_bias,
    outer_pair_weight,
    stored_lhs_operand,
    stored_rhs_operand,
    left_projection_weight,
    right_projection_weight,
    outer_mean_norm_gain,
    transition_norm_gain,
    gate_weight,
    up_weight,
    down_weight,
    side_stack_entry,
    arriving_stack_derivative,
):
    rows, cols, _ = pair_activation.shape
    width, bins = distogram_weight.shape
    factor_width = stored_lhs_operand.shape[1]
    features = left_projection_weight.shape[0]
    row_devices = lax.axis_size("row")
    col_devices = lax.axis_size("col")
    parts = row_devices // col_devices
    seqs = stored_lhs_operand.shape[0] * row_devices
    part = (lax.axis_index("row") % parts).astype(jnp.int32)[None]
    weight_t = distogram_weight.T
    bias = distogram_bias[:, None]
    same = jnp.eye(GROUP, dtype=BF16)
    weight_wide = (same[:, None, :, None] * weight_t[None, :, None, :]).reshape(
        GROUP * bins, GROUP * width
    )

    factors = jnp.swapaxes(jnp.concatenate([stored_rhs_operand, stored_lhs_operand], axis=1), 0, 1)
    factors = lax.all_gather(factors, "row", axis=1, tiled=True)
    factors = factors.reshape(2 * factor_width * seqs, cols)

    chunks = chunk_plan(rows)
    leg_pairs = first_leg(col_devices, parts)
    received = []
    for first_row, chunk_rows in chunks:
        pieces = [
            mirror_logits(
                part, pair_activation, weight_t, bias, first_row, chunk_rows, shift, parts
            )
            for shift in range(parts)
        ]
        relayed = [lax.ppermute(piece, AXES, leg_pairs) for piece in pieces]
        received.append(
            [
                lax.ppermute(piece, AXES, second_leg(col_devices, parts, shift))
                for shift, piece in enumerate(relayed)
            ]
        )

    outer_weight = outer_pair_weight.astype(F32).reshape(factor_width, factor_width, width)
    by_bin = jnp.einsum(
        "pb,cep->bce", distogram_weight.astype(F32), outer_weight, precision=lax.Precision.HIGHEST
    )
    mix_right = jnp.einsum(
        "mc,bce->ebm", left_projection_weight.astype(F32), by_bin, precision=lax.Precision.HIGHEST
    )
    mix_left = jnp.einsum(
        "me,bce->cbm", right_projection_weight.astype(F32), by_bin, precision=lax.Precision.HIGHEST
    )
    mix = (jnp.concatenate([mix_right, mix_left], axis=0) / seqs).astype(BF16)
    mix = jnp.concatenate([mix, mix], axis=2)

    devices = row_devices * col_devices
    grad = ()
    norm_parts = []
    for (first_row, chunk_rows), pieces in zip(chunks, received):
        *grad, norm_part = pair_step(
            part, pair_activation, pieces, target_distance_bins, weight_t, weight_wide, bias,
            factors, mix, grad, first_row, seqs, devices,
        )
        norm_parts.append(norm_part)
    early = jnp.concatenate(norm_parts[:-1], axis=1) if len(chunks) > 2 else norm_parts[0]
    sent = [early] + norm_parts[1:][-1:] if len(chunks) > 1 else [early]
    arrived = [lax.all_to_all(x, AXES, split_axis=0, concat_axis=0, tiled=True) for x in sent]
    pieces = []
    for n, part_sums in enumerate(norm_parts):
        last = n == len(chunks) - 1 and n > 0
        at = 0 if last else sum(x.shape[1] for x in norm_parts[:n])
        pieces.append((int(last), at, chunks[n][1] // GROUP))
    alignment_gradient = transition(
        side_stack_entry, arriving_stack_derivative, arrived, pieces, rows, col_devices,
        outer_mean_norm_gain, transition_norm_gain, gate_weight, up_weight, down_weight,
    )
    return grad[0], alignment_gradient


def solution(mesh):
    return jax.shard_map(
        per_device,
        mesh=mesh,
        in_specs=(
            P("row", "col", None),
            P("row", "col"),
            P(),
            P(),
            P(),
            P("row", None, "col"),
            P("row", None, "col"),
            P(),
            P(),
            P(),
            P(),
            P(),
            P(),
            P(),
            P(AXES, None, None),
            P(AXES, None, None),
        ),
        out_specs=(P("row", "col", None), P(AXES, None, None)),
        check_vma=False,
    )
```

```python
import functools

import jax
import jax.numpy as jnp
from jax import lax
from jax.experimental import pallas as pl
from jax.experimental.pallas import tpu as pltpu
from jax.sharding import PartitionSpec as P

BF16, F32 = jnp.bfloat16, jnp.float32
VMEM_BYTES = 56 * 1024 * 1024
AXES = ("row", "col")
GROUP = 4


def contract(lhs, rhs, lhs_dim, rhs_dim):
    return lax.dot_general(
        lhs, rhs, (((lhs_dim,), (rhs_dim,)), ((), ())), preferred_element_type=F32
    )


def relay(block, z, blocks):
    if blocks % 4:
        return z, block
    low_block = ((1 - (block & 1)) << 1) | (z & 1)
    low_z = (z & 2) | ((block >> 1) & 1)
    return (z >> 2 << 2) | low_block, (block >> 2 << 2) | low_z


def first_leg(blocks, parts):
    pairs = []
    for block in range(blocks):
        for z in range(blocks):
            to_block, to_z = relay(block, z, blocks)
            for h in range(parts):
                pairs.append(
                    ((block * parts + h) * blocks + z, (to_block * parts + h) * blocks + to_z)
                )
    return pairs


def second_leg(blocks, parts, shift):
    pairs = []
    for block in range(blocks):
        for z in range(blocks):
            via_block, via_z = relay(block, z, blocks)
            for h in range(parts):
                pairs.append(
                    (
                        (via_block * parts + h) * blocks + via_z,
                        (z * parts + (h + shift) % parts) * blocks + block,
                    )
                )
    return pairs


def as_column(row):
    n = row.shape[1]
    across = lax.broadcasted_iota(jnp.int32, (n, n), 0)
    along = lax.broadcasted_iota(jnp.int32, (n, n), 1)
    return jnp.sum(jnp.where(across == along, row, 0.0), axis=1, keepdims=True)


def mirror_logits_kernel(part_ref, pair_ref, weight_ref, bias_ref, *refs):
    out_ref, widened = refs[-2:]
    own_rows, step_cols, width = pair_ref.shape
    widened[...] = pair_ref[...].astype(F32).reshape(own_rows * step_cols, width)
    weight = weight_ref[...]
    bias = as_column(bias_ref[...])
    for j in range(step_cols):
        column = widened[pl.ds(j, own_rows, stride=step_cols), :].astype(BF16)
        out_ref[0, j] = (contract(weight, column, 1, 1) + bias).astype(BF16)


def mirror_logits(part, pair_activation, weight_t, bias, first_row, chunk_rows, parts, ahead):
    rows, cols, width = pair_activation.shape
    bins = weight_t.shape[0]
    step = min(16, chunk_rows)
    steps = chunk_rows // step

    def block(s, part_ref):
        half = lax.rem(part_ref[0] + s // steps, parts)
        return (0, half * (rows // step) + first_row // step + lax.rem(s, steps), 0)

    return pl.pallas_call(
        mirror_logits_kernel,
        grid_spec=pltpu.PrefetchScalarGridSpec(
            num_scalar_prefetch=1,
            grid=(parts * steps,),
            in_specs=[
                pl.BlockSpec((rows, step, width), block),
                pl.BlockSpec((bins, width), lambda s, p: (0, 0)),
                pl.BlockSpec((1, bins), lambda s, p: (0, 0)),
            ]
            + [pl.BlockSpec(memory_space=pl.ANY)] * len(ahead),
            out_specs=pl.BlockSpec(
                (1, step, bins, rows), lambda s, p: (s // steps, lax.rem(s, steps), 0, 0)
            ),
            scratch_shapes=[pltpu.VMEM((rows * step, width), F32)],
        ),
        out_shape=jax.ShapeDtypeStruct((parts, chunk_rows, bins, rows), BF16),
        compiler_params=pltpu.CompilerParams(vmem_limit_bytes=VMEM_BYTES),
        cost_estimate=pl.CostEstimate(
            flops=2 * parts * chunk_rows * rows * bins * width * 4,
            bytes_accessed=parts * chunk_rows * rows * (width + bins) * 2,
            transcendentals=0,
        ),
        name="mirror_logits",
    )(part, pair_activation, weight_t, bias, *ahead)


def split_kernel(in_ref, *outs):
    for n, out_ref in enumerate(outs):
        out_ref[...] = in_ref[n]


def split(array):
    count, rows, *rest = array.shape
    step = min(16, rows)
    return pl.pallas_call(
        split_kernel,
        grid=(rows // step,),
        in_specs=[pl.BlockSpec((count, step, *rest), lambda s: (0, s, 0, 0))],
        out_specs=[pl.BlockSpec((step, *rest), lambda s: (s, 0, 0))] * count,
        out_shape=[jax.ShapeDtypeStruct(array.shape[1:], array.dtype)] * count,
        compiler_params=pltpu.CompilerParams(vmem_limit_bytes=VMEM_BYTES),
        name="split",
    )(array)


def join_kernel(axis, count, *refs):
    out_ref = refs[-1]
    width = refs[0].shape[axis]
    for n, ref in enumerate(refs[:count]):
        if axis:
            out_ref[:, n * width : (n + 1) * width] = ref[...]
        else:
            out_ref[n * width : (n + 1) * width] = ref[...]


def join(arrays, axis, ahead=()):
    shape = list(arrays[0].shape)
    shape[axis] *= len(arrays)
    vmem = pl.BlockSpec(memory_space=pltpu.VMEM)
    return pl.pallas_call(
        functools.partial(join_kernel, axis, len(arrays)),
        in_specs=[vmem] * len(arrays) + [pl.BlockSpec(memory_space=pl.ANY)] * len(ahead),
        out_specs=vmem,
        out_shape=jax.ShapeDtypeStruct(shape, BF16),
        compiler_params=pltpu.CompilerParams(vmem_limit_bytes=VMEM_BYTES),
        name="join",
    )(*arrays, *ahead)


def pair_kernel(parts, slots, front, tile, part_ref, pair_ref, *refs):
    received = refs[:parts]
    target_ref, weight_t_ref, weight_wide_ref, bias_ref, factor_hbm, mix_hbm = refs[parts : parts + 6]
    grad_ref, norm_ref, slopes, factors, mix, mix_wide, mixed, total, sems = refs[-9:]
    step = pl.program_id(0)
    step_rows, cols, width = pair_ref.shape
    bins = weight_t_ref.shape[0]
    groups = slopes.shape[0]
    step_groups = step_rows // GROUP
    features = total.shape[0] * total.shape[2] // GROUP
    devices, device_rows, _ = norm_ref.shape
    device_seqs = device_rows // groups
    seqs = devices * device_seqs
    xs = mix.shape[0]
    copies = [
        pltpu.make_async_copy(factor_hbm, factors, sems.at[0]),
        pltpu.make_async_copy(mix_hbm, mix, sems.at[1]),
    ]

    @pl.when(step == 0)
    def _():
        for copy in copies:
            copy.start()
        total[...] = jnp.zeros_like(total)
        mix_wide[...] = jnp.zeros_like(mix_wide)

    @pl.when(step < front)
    def _():
        h = part_ref[0]
        weight_t = weight_t_ref[...]
        bias = as_column(bias_ref[...])
        levels = lax.broadcasted_iota(jnp.int32, (bins, cols), 0)
        for g in range(step_groups):
            group = []
            for r in range(GROUP):
                i = g * GROUP + r
                own = (contract(weight_t, pair_ref[i], 1, 1) + bias).astype(BF16).astype(F32)
                halves = []
                for u in range(parts):
                    half = received[0][i]
                    for shift in range(1, parts):
                        half = jnp.where(
                            lax.rem(h + parts - u, parts) == shift, received[shift][i], half
                        )
                    halves.append(half)
                symmetric = own + jnp.concatenate(halves, axis=1).astype(F32)
                top = jnp.max(symmetric, axis=0, keepdims=True)
                raised = jnp.exp(symmetric - top)
                scale = 2.0 / jnp.sum(raised, axis=0, keepdims=True)
                hit = jnp.where(levels == target_ref[i : i + 1, :], 2.0, 0.0)
                group.append((raised * scale - hit).astype(BF16))
            slope = jnp.concatenate(group, axis=0).T
            slopes[step * step_groups + g] = slope
            out = contract(slope, weight_wide_ref[...], 1, 0).astype(BF16)
            for r in range(GROUP):
                grad_ref[g * GROUP + r] = out[:, r * width : (r + 1) * width]

    @pl.when(step == front)
    def _():
        for copy in copies:
            copy.wait()
        half_groups = max(1, groups // 2)

        def add_tile(t, carry):
            for x in range(tile):
                for r in range(GROUP):
                    rows = pl.ds((x * GROUP + r) * bins, bins)
                    at = r * features
                    mix_wide[rows, at : at + features] = (
                        mix[t * tile + x, :, at % 128 : at % 128 + features]
                    )
            factor = factors[pl.ds(pl.multiple_of(t * tile * seqs, tile * seqs), tile * seqs), :]
            for g in range(groups):
                spread = contract(factor, slopes[g], 1, 0).astype(BF16)
                for x in range(tile):
                    mixed[g * seqs : (g + 1) * seqs, x * GROUP * bins : (x + 1) * GROUP * bins] = (
                        spread[x * seqs : (x + 1) * seqs, :]
                    )
            for g in range(0, groups, half_groups):
                rows = slice(g * seqs, (g + half_groups) * seqs)
                term = contract(mixed[rows, :], mix_wide[...], 1, 0)
                for c in range(total.shape[0]):
                    total[c, rows, :] += term[:, c * 128 : (c + 1) * 128]
            return carry

        lax.fori_loop(0, xs // tile, add_tile, 0)
        slot_seqs = seqs // slots
        for s in range(seqs):
            slot, rest = divmod(s, slot_seqs)
            device, k = divmod(rest, device_seqs)
            other, pair = divmod(slot, slots // parts)
            block = part_ref[1] ^ pair
            device += (block * parts + lax.rem(part_ref[0] + other, parts)) * (devices // slots)
            for c in range(total.shape[0]):
                norm_ref[device, k * groups : (k + 1) * groups, c * 128 : (c + 1) * 128] = (
                    total[c, pl.ds(s, groups, stride=seqs), :].astype(BF16)
                )


def pair_step(
    part, pair_activation, received, targets, weight_t, weight_wide, bias, factors, mix, grad,
    first_row, seqs, devices, slots, ahead,
):
    _, cols, width = pair_activation.shape
    bins = weight_t.shape[0]
    features = mix.shape[2] // 2
    parts = len(received)
    chunk_rows = received[0].shape[0]
    step_rows = min(16, chunk_rows)
    groups = chunk_rows // GROUP
    xs = factors.shape[0] // seqs
    tile = max(1, min(8, 512 // seqs))
    front = chunk_rows // step_rows
    near = lambda s: jnp.minimum(s, front - 1)
    there = lambda s: first_row // step_rows + jnp.minimum(s, front - 1)
    const2 = lambda s, p: (0, 0)
    norm_shape = (devices, seqs // devices * groups, GROUP * features)
    return pl.pallas_call(
        functools.partial(pair_kernel, parts, slots, front, tile),
        grid_spec=pltpu.PrefetchScalarGridSpec(
            num_scalar_prefetch=1,
            grid=(front + 1,),
            in_specs=[pl.BlockSpec((step_rows, cols, width), lambda s, p: (there(s), 0, 0))]
            + [pl.BlockSpec((step_rows, bins, cols // parts), lambda s, p: (near(s), 0, 0))] * parts
            + [
                pl.BlockSpec((step_rows, cols), lambda s, p: (there(s), 0)),
                pl.BlockSpec((bins, width), const2),
                pl.BlockSpec((GROUP * bins, GROUP * width), const2),
                pl.BlockSpec((1, bins), const2),
            ]
            + [pl.BlockSpec(memory_space=pl.ANY)] * (2 + len(grad) + len(ahead)),
            out_specs=[
                pl.BlockSpec((step_rows, cols, width), lambda s, p: (there(s), 0, 0)),
                pl.BlockSpec(norm_shape, lambda s, p: (0, 0, 0)),
            ],
            scratch_shapes=[
                pltpu.VMEM((groups, cols, GROUP * bins), BF16),
                pltpu.VMEM(factors.shape, BF16),
                pltpu.VMEM(mix.shape, BF16),
                pltpu.VMEM((tile * GROUP * bins, GROUP * features), BF16),
                pltpu.VMEM((groups * seqs, tile * GROUP * bins), BF16),
                pltpu.VMEM((GROUP * features // 128, groups * seqs, 128), F32),
                pltpu.SemaphoreType.DMA((2,)),
            ],
        ),
        out_shape=[
            jax.ShapeDtypeStruct(pair_activation.shape, BF16),
            jax.ShapeDtypeStruct(norm_shape, BF16),
        ],
        input_output_aliases={parts + 8: 0} if grad else {},
        compiler_params=pltpu.CompilerParams(vmem_limit_bytes=VMEM_BYTES),
        cost_estimate=pl.CostEstimate(
            flops=4 * xs * seqs * cols * chunk_rows * bins,
            bytes_accessed=chunk_rows * cols * width * 6,
            transcendentals=chunk_rows * cols * bins,
        ),
        name="pair_step",
    )(part, pair_activation, *received, targets, weight_t, weight_wide, bias, factors, mix, *grad,
      *ahead)


def norm_forward(features):
    centered = features - jnp.mean(features, axis=0, keepdims=True)
    scale_inv = lax.rsqrt(jnp.mean(centered * centered, axis=0, keepdims=True) + 1e-05)
    return centered * scale_inv, scale_inv


def norm_backward(incoming, normed, scale_inv):
    first_mean = jnp.mean(incoming, axis=0, keepdims=True)
    second_mean = jnp.mean(incoming * normed, axis=0, keepdims=True)
    return scale_inv * (incoming - first_mean - normed * second_mean)


def transition_kernel(
    pieces, rows, col_devices, entry_ref, arriving_ref, mean_gain_ref, gain_ref, gate_up_t_ref,
    gate_up_ref, down_ref, down_t_ref, *refs,
):
    arrived, (out_ref, incoming) = refs[:-2], refs[-2:]
    hidden = down_ref.shape[0]
    seqs, features, positions = out_ref.shape
    groups = rows // GROUP
    row = lax.broadcasted_iota(jnp.int32, (groups, rows), 0)
    col = lax.broadcasted_iota(jnp.int32, (groups, rows), 1)
    spread = [jnp.where(col == GROUP * row + r, 1.0, 0.0).astype(BF16) for r in range(GROUP)]

    for s in range(seqs):
        for block in range(positions // rows):
            sums = []
            for which, at, count in pieces:
                at += s * count
                sums.append(
                    sum(
                        arrived[which][block * col_devices + c, at : at + count, :].astype(F32)
                        for c in range(col_devices)
                    )
                )
            field = jnp.concatenate(sums, axis=0).astype(BF16)
            incoming[s, :, block * rows : (block + 1) * rows] = sum(
                contract(field[:, r * features : (r + 1) * features], spread[r], 0, 0)
                for r in range(GROUP)
            )

    gain = gain_ref[...]
    for s in range(seqs):
        entry = entry_ref[s].astype(F32)
        normed, scale_inv = norm_forward(entry)
        normed_input = (normed * gain).astype(BF16)
        both = contract(gate_up_t_ref[...], normed_input, 1, 0)
        gate, up = both[:hidden], both[hidden:]
        sig = jax.nn.sigmoid(gate)
        silu = gate * sig
        msa_out = entry + contract(down_t_ref[...], (silu * up).astype(BF16), 1, 0)
        second_normed, second_scale = norm_forward(msa_out)
        middle = arriving_ref[s].astype(F32) + norm_backward(
            incoming[s] * mean_gain_ref[...], second_normed, second_scale
        )
        hidden_grad = contract(down_ref[...], middle.astype(BF16), 1, 0)
        gate_grad = (hidden_grad * up * sig * (1.0 + gate * (1.0 - sig))).astype(BF16)
        up_grad = (hidden_grad * silu).astype(BF16)
        normed_grad = contract(
            gate_up_ref[...], jnp.concatenate([gate_grad, up_grad], axis=0), 1, 0
        )
        out = middle + norm_backward(normed_grad * gain, normed, scale_inv)
        out_ref[s] = out.astype(BF16)


def transition(
    entry, arriving, arrived, pieces, rows, col_devices, mean_gain, gain, gate_weight, up_weight,
    down_weight,
):
    features = entry.shape[1]
    gate_up = jnp.concatenate([gate_weight, up_weight], axis=1)
    return pl.pallas_call(
        functools.partial(transition_kernel, pieces, rows, col_devices),
        out_shape=jax.ShapeDtypeStruct(entry.shape, BF16),
        scratch_shapes=[pltpu.VMEM(entry.shape, F32)],
        compiler_params=pltpu.CompilerParams(vmem_limit_bytes=VMEM_BYTES),
        name="transition",
    )(entry, arriving, mean_gain[:, None], gain[:, None], gate_up.T, gate_up, down_weight,
      down_weight.T, *arrived)


def chunk_plan(rows):
    size = max(16, rows // 4)
    return [(at, min(size, rows - at)) for at in range(0, rows, size)]


def per_device(
    pair_activation,
    target_distance_bins,
    distogram_weight,
    distogram_bias,
    outer_pair_weight,
    stored_lhs_operand,
    stored_rhs_operand,
    left_projection_weight,
    right_projection_weight,
    outer_mean_norm_gain,
    transition_norm_gain,
    gate_weight,
    up_weight,
    down_weight,
    side_stack_entry,
    arriving_stack_derivative,
):
    rows, cols, _ = pair_activation.shape
    width, bins = distogram_weight.shape
    factor_width = stored_lhs_operand.shape[1]
    features = left_projection_weight.shape[0]
    row_devices = lax.axis_size("row")
    col_devices = lax.axis_size("col")
    parts = row_devices // col_devices
    seqs = stored_lhs_operand.shape[0] * row_devices
    row_index = lax.axis_index("row").astype(jnp.int32)
    part = jnp.stack([row_index % parts, row_index // parts])
    weight_t = distogram_weight.T
    bias = distogram_bias[None, :]
    same = jnp.eye(GROUP, dtype=BF16)
    weight_wide = (same[:, None, :, None] * weight_t[None, :, None, :]).reshape(
        GROUP * bins, GROUP * width
    )

    blocks = row_devices // parts
    own = join([stored_rhs_operand, stored_lhs_operand], 1)
    others = []
    for flip in range(1, blocks):
        pairs = [((n ^ flip) * parts + h, n * parts + h) for n in range(blocks) for h in range(parts)]
        others.append(lax.ppermute(own, "row", pairs))

    chunks = chunk_plan(rows)
    leg_pairs = first_leg(col_devices, parts)
    logits, relayed, received = [], [], []
    for first_row, chunk_rows in chunks:
        n = len(logits)
        ahead = [x for arrays in logits[-1:] + relayed[: max(0, n - 1)][-1:] for x in arrays]
        if n == 1:
            ahead += others
        pieces = mirror_logits(
            part, pair_activation, weight_t, bias, first_row, chunk_rows, parts, ahead
        )
        logits.append([pieces])
        relayed.append(split(lax.ppermute(pieces, AXES, leg_pairs)))
        received.append(
            [
                lax.ppermute(piece, AXES, second_leg(col_devices, parts, shift))
                for shift, piece in enumerate(relayed[-1])
            ]
        )

    across = join([own] + others, 0)
    shifted = [across]
    for shift in range(1, parts):
        pairs = [
            (n * parts + (h + shift) % parts, n * parts + h)
            for n in range(blocks) for h in range(parts)
        ]
        shifted.append(lax.ppermute(across, "row", pairs))
    factors = jnp.concatenate(shifted).reshape(seqs, 2 * factor_width, cols)
    factors = factors.swapaxes(0, 1).reshape(2 * factor_width * seqs, cols)

    outer_weight = outer_pair_weight.astype(F32).reshape(factor_width, factor_width, width)
    by_bin = jnp.einsum(
        "pb,cep->bce", distogram_weight.astype(F32), outer_weight, precision=lax.Precision.HIGHEST
    )
    mix_right = jnp.einsum(
        "mc,bce->ebm", left_projection_weight.astype(F32), by_bin, precision=lax.Precision.HIGHEST
    )
    mix_left = jnp.einsum(
        "me,bce->cbm", right_projection_weight.astype(F32), by_bin, precision=lax.Precision.HIGHEST
    )
    mix = (jnp.concatenate([mix_right, mix_left], axis=0) / seqs).astype(BF16)
    mix = jnp.concatenate([mix, mix], axis=2)

    devices = row_devices * col_devices
    grad = ()
    norm_parts = []
    exchange = functools.partial(
        lax.all_to_all, axis_name=AXES, split_axis=0, concat_axis=0, tiled=True
    )
    arrived = []
    for n, ((first_row, chunk_rows), pieces) in enumerate(zip(chunks, received)):
        ahead = [x for arrays in logits[n + 2 : n + 3] + relayed[n + 1 : n + 2] for x in arrays]
        if n == len(chunks) - 1 and n > 0:
            early = join(norm_parts, 1, pieces)
            arrived.append(exchange(early))
            ahead.append(early)
        *grad, norm_part = pair_step(
            part, pair_activation, pieces, target_distance_bins, weight_t, weight_wide, bias,
            factors, mix, grad, first_row, seqs, devices, row_devices, ahead,
        )
        norm_parts.append(norm_part)
    final = norm_parts[-1]
    if arrived:
        final, arrived[0] = lax.optimization_barrier((final, arrived[0]))
    arrived.append(exchange(final))
    pieces = []
    for n, part_sums in enumerate(norm_parts):
        last = n == len(chunks) - 1 and n > 0
        at = 0 if last else sum(x.shape[1] for x in norm_parts[:n])
        pieces.append((int(last), at, chunks[n][1] // GROUP))
    alignment_gradient = transition(
        side_stack_entry, arriving_stack_derivative, arrived, pieces, rows, col_devices,
        outer_mean_norm_gain, transition_norm_gain, gate_weight, up_weight, down_weight,
    )
    return grad[0], alignment_gradient


def solution(mesh):
    return jax.shard_map(
        per_device,
        mesh=mesh,
        in_specs=(
            P("row", "col", None),
            P("row", "col"),
            P(),
            P(),
            P(),
            P("row", None, "col"),
            P("row", None, "col"),
            P(),
            P(),
            P(),
            P(),
            P(),
            P(),
            P(),
            P(AXES, None, None),
            P(AXES, None, None),
        ),
        out_specs=(P("row", "col", None), P(AXES, None, None)),
        check_vma=False,
    )
```

```python
import functools

import jax
import jax.numpy as jnp
from jax import lax
from jax.experimental import pallas as pl
from jax.experimental.pallas import tpu as pltpu
from jax.sharding import PartitionSpec as P

BF16, F32 = jnp.bfloat16, jnp.float32
VMEM_BYTES = 56 * 1024 * 1024
LEAN_BYTES = 32 * 1024 * 1024
AXES = ("row", "col")
GROUP = 4
SHORT = pl.CostEstimate(flops=0, bytes_accessed=0, transcendentals=0)


def contract(lhs, rhs, lhs_dim, rhs_dim):
    return lax.dot_general(
        lhs, rhs, (((lhs_dim,), (rhs_dim,)), ((), ())), preferred_element_type=F32
    )


def relay(block, z, blocks):
    if blocks % 4:
        return z, block
    low_block = ((1 - (block & 1)) << 1) | (z & 1)
    low_z = (z & 2) | ((block >> 1) & 1)
    return (z >> 2 << 2) | low_block, (block >> 2 << 2) | low_z


def first_leg(blocks, parts):
    pairs = []
    for block in range(blocks):
        for z in range(blocks):
            to_block, to_z = relay(block, z, blocks)
            for h in range(parts):
                pairs.append(
                    ((block * parts + h) * blocks + z, (to_block * parts + h) * blocks + to_z)
                )
    return pairs


def second_leg(blocks, parts, shift):
    pairs = []
    for block in range(blocks):
        for z in range(blocks):
            via_block, via_z = relay(block, z, blocks)
            for h in range(parts):
                pairs.append(
                    (
                        (via_block * parts + h) * blocks + via_z,
                        (z * parts + (h + shift) % parts) * blocks + block,
                    )
                )
    return pairs


def as_column(row):
    n = row.shape[1]
    across = lax.broadcasted_iota(jnp.int32, (n, n), 0)
    along = lax.broadcasted_iota(jnp.int32, (n, n), 1)
    return jnp.sum(jnp.where(across == along, row, 0.0), axis=1, keepdims=True)


def mirror_logits_kernel(part_ref, pair_ref, weight_ref, bias_ref, *refs):
    out_ref, widened = refs[-2:]
    own_rows, step_cols, width = pair_ref.shape
    widened[...] = pair_ref[...].astype(F32).reshape(own_rows * step_cols, width)
    weight = weight_ref[...]
    bias = as_column(bias_ref[...])
    for j in range(step_cols):
        column = widened[pl.ds(j, own_rows, stride=step_cols), :].astype(BF16)
        out_ref[0, j] = (contract(weight, column, 1, 1) + bias).astype(BF16)


def mirror_logits(part, pair_activation, weight_t, bias, first_row, chunk_rows, parts, ahead):
    rows, cols, width = pair_activation.shape
    bins = weight_t.shape[0]
    step = min(16, chunk_rows)
    steps = chunk_rows // step

    def block(s, part_ref):
        half = lax.rem(part_ref[0] + s // steps, parts)
        return (0, half * (rows // step) + first_row // step + lax.rem(s, steps), 0)

    return pl.pallas_call(
        mirror_logits_kernel,
        grid_spec=pltpu.PrefetchScalarGridSpec(
            num_scalar_prefetch=1,
            grid=(parts * steps,),
            in_specs=[
                pl.BlockSpec((rows, step, width), block),
                pl.BlockSpec((bins, width), lambda s, p: (0, 0)),
                pl.BlockSpec((1, bins), lambda s, p: (0, 0)),
            ]
            + [pl.BlockSpec(memory_space=pl.ANY)] * len(ahead),
            out_specs=pl.BlockSpec(
                (1, step, bins, rows), lambda s, p: (s // steps, lax.rem(s, steps), 0, 0)
            ),
            scratch_shapes=[pltpu.VMEM((rows * step, width), F32)],
        ),
        out_shape=jax.ShapeDtypeStruct((parts, chunk_rows, bins, rows), BF16),
        compiler_params=pltpu.CompilerParams(vmem_limit_bytes=VMEM_BYTES),
        cost_estimate=SHORT,
        name="mirror_logits",
    )(part, pair_activation, weight_t, bias, *ahead)


def tie_kernel(*refs):
    pass


def tie(array, ahead):
    anywhere = pl.BlockSpec(memory_space=pl.ANY)
    return pl.pallas_call(
        tie_kernel,
        in_specs=[anywhere] * (1 + len(ahead)),
        out_specs=anywhere,
        out_shape=jax.ShapeDtypeStruct(array.shape, array.dtype),
        input_output_aliases={0: 0},
        compiler_params=pltpu.CompilerParams(vmem_limit_bytes=LEAN_BYTES),
        name="tie",
    )(array, *ahead)


def split_kernel(in_ref, *refs):
    for n, out_ref in enumerate(refs[-in_ref.shape[0] :]):
        out_ref[...] = in_ref[n]


def split(array, ahead):
    count, rows, *rest = array.shape
    step = min(16, rows)
    return pl.pallas_call(
        split_kernel,
        grid=(rows // step,),
        in_specs=[pl.BlockSpec((count, step, *rest), lambda s: (0, s, 0, 0))]
        + [pl.BlockSpec(memory_space=pl.ANY)] * len(ahead),
        out_specs=[pl.BlockSpec((step, *rest), lambda s: (s, 0, 0))] * count,
        out_shape=[jax.ShapeDtypeStruct(array.shape[1:], array.dtype)] * count,
        compiler_params=pltpu.CompilerParams(vmem_limit_bytes=LEAN_BYTES),
        name="split",
    )(array, *ahead)


def join_kernel(axis, count, *refs):
    out_ref = refs[-1]
    at = 0
    for ref in refs[:count]:
        end = at + ref.shape[axis]
        if axis:
            out_ref[:, at:end] = ref[...]
        else:
            out_ref[at:end] = ref[...]
        at = end


def join(arrays, axis, ahead=()):
    shape = list(arrays[0].shape)
    shape[axis] = sum(array.shape[axis] for array in arrays)
    vmem = pl.BlockSpec(memory_space=pltpu.VMEM)
    return pl.pallas_call(
        functools.partial(join_kernel, axis, len(arrays)),
        in_specs=[vmem] * len(arrays) + [pl.BlockSpec(memory_space=pl.ANY)] * len(ahead),
        out_specs=vmem,
        out_shape=jax.ShapeDtypeStruct(shape, BF16),
        compiler_params=pltpu.CompilerParams(vmem_limit_bytes=LEAN_BYTES),
        name="join",
    )(*arrays, *ahead)


def pair_kernel(parts, slots, front, tile, resident, part_ref, pair_ref, *refs):
    received = refs[:parts]
    target_ref, weight_t_ref, weight_wide_ref, bias_ref, factors, mix = refs[parts : parts + 6]
    if resident:
        grad_ref, norm_ref, slopes, mix_wide, mixed, total = refs[-6:]
        copies = []
    else:
        grad_ref, norm_ref, slopes, mix_wide, mixed, total, factor_copy, mix_copy, sems = refs[-9:]
        copies = [
            pltpu.make_async_copy(factors, factor_copy, sems.at[0]),
            pltpu.make_async_copy(mix, mix_copy, sems.at[1]),
        ]
        factors, mix = factor_copy, mix_copy
    step = pl.program_id(0)
    step_rows, cols, width = pair_ref.shape
    bins = weight_t_ref.shape[0]
    groups = slopes.shape[0]
    step_groups = step_rows // GROUP
    features = total.shape[0] * total.shape[2] // GROUP
    devices, device_rows, _ = norm_ref.shape
    device_seqs = device_rows // groups
    seqs = devices * device_seqs
    xs = mix.shape[0]
    base = step * step_rows if resident else 0

    @pl.when(step == 0)
    def _():
        for copy in copies:
            copy.start()
        total[...] = jnp.zeros_like(total)
        mix_wide[...] = jnp.zeros_like(mix_wide)

    @pl.when(step < front)
    def _():
        h = part_ref[0]
        weight_t = weight_t_ref[...]
        bias = as_column(bias_ref[...])
        levels = lax.broadcasted_iota(jnp.int32, (bins, cols), 0)
        for g in range(step_groups):
            group = []
            for r in range(GROUP):
                i = g * GROUP + r
                own = (contract(weight_t, pair_ref[i], 1, 1) + bias).astype(BF16).astype(F32)
                halves = []
                for u in range(parts):
                    half = received[0][base + i]
                    for shift in range(1, parts):
                        half = jnp.where(
                            lax.rem(h + parts - u, parts) == shift, received[shift][base + i], half
                        )
                    halves.append(half)
                symmetric = own + jnp.concatenate(halves, axis=1).astype(F32)
                top = jnp.max(symmetric, axis=0, keepdims=True)
                raised = jnp.exp(symmetric - top)
                scale = 2.0 / jnp.sum(raised, axis=0, keepdims=True)
                hit = jnp.where(levels == target_ref[i : i + 1, :], 2.0, 0.0)
                group.append((raised * scale - hit).astype(BF16))
            slope = jnp.concatenate(group, axis=0).T
            slopes[step * step_groups + g] = slope
            out = contract(slope, weight_wide_ref[...], 1, 0).astype(BF16)
            for r in range(GROUP):
                grad_ref[g * GROUP + r] = out[:, r * width : (r + 1) * width]

    @pl.when(step == front)
    def _():
        for copy in copies:
            copy.wait()
        half_groups = max(1, groups // 2)

        def add_tile(t, carry):
            for x in range(tile):
                for r in range(GROUP):
                    rows = pl.ds((x * GROUP + r) * bins, bins)
                    at = r * features
                    mix_wide[rows, at : at + features] = (
                        mix[t * tile + x, :, at % 128 : at % 128 + features]
                    )
            factor = factors[pl.ds(pl.multiple_of(t * tile * seqs, tile * seqs), tile * seqs), :]
            for g in range(groups):
                spread = contract(factor, slopes[g], 1, 0).astype(BF16)
                for x in range(tile):
                    mixed[g * seqs : (g + 1) * seqs, x * GROUP * bins : (x + 1) * GROUP * bins] = (
                        spread[x * seqs : (x + 1) * seqs, :]
                    )
            for g in range(0, groups, half_groups):
                rows = slice(g * seqs, (g + half_groups) * seqs)
                term = contract(mixed[rows, :], mix_wide[...], 1, 0)
                for c in range(total.shape[0]):
                    total[c, rows, :] += term[:, c * 128 : (c + 1) * 128]
            return carry

        lax.fori_loop(0, xs // tile, add_tile, 0)
        slot_seqs = seqs // slots
        for s in range(seqs):
            slot, rest = divmod(s, slot_seqs)
            device, k = divmod(rest, device_seqs)
            other, pair = divmod(slot, slots // parts)
            block = part_ref[1] ^ pair
            device += (block * parts + lax.rem(part_ref[0] + other, parts)) * (devices // slots)
            for c in range(total.shape[0]):
                norm_ref[device, k * groups : (k + 1) * groups, c * 128 : (c + 1) * 128] = (
                    total[c, pl.ds(s, groups, stride=seqs), :].astype(BF16)
                )


def pair_step(
    part, pair_activation, received, targets, weight_t, weight_wide, bias, factors, mix, grad,
    first_row, seqs, devices, slots, ahead, resident,
):
    _, cols, width = pair_activation.shape
    bins = weight_t.shape[0]
    features = mix.shape[2] // 2
    parts = len(received)
    chunk_rows = received[0].shape[0]
    step_rows = min(16, chunk_rows)
    groups = chunk_rows // GROUP
    xs = factors.shape[0] // seqs
    tile = max(1, min(8, 512 // seqs))
    front = chunk_rows // step_rows
    near = lambda s: jnp.minimum(s, front - 1)
    anywhere = pl.BlockSpec(memory_space=pl.ANY)
    if resident:
        held = moved = pl.BlockSpec(memory_space=pltpu.VMEM)
    else:
        held = pl.BlockSpec((step_rows, bins, cols // parts), lambda s, p: (near(s), 0, 0))
        moved = anywhere
    there = lambda s: first_row // step_rows + jnp.minimum(s, front - 1)
    const2 = lambda s, p: (0, 0)
    norm_shape = (devices, seqs // devices * groups, GROUP * features)
    return pl.pallas_call(
        functools.partial(pair_kernel, parts, slots, front, tile, resident),
        grid_spec=pltpu.PrefetchScalarGridSpec(
            num_scalar_prefetch=1,
            grid=(front + 1,),
            in_specs=[pl.BlockSpec((step_rows, cols, width), lambda s, p: (there(s), 0, 0))]
            + [held] * parts
            + [
                pl.BlockSpec((step_rows, cols), lambda s, p: (there(s), 0)),
                pl.BlockSpec((bins, width), const2),
                pl.BlockSpec((GROUP * bins, GROUP * width), const2),
                pl.BlockSpec((1, bins), const2),
            ]
            + [moved] * 2
            + [pl.BlockSpec(memory_space=pltpu.HBM)] * len(grad)
            + [anywhere] * len(ahead),
            out_specs=[
                pl.BlockSpec((step_rows, cols, width), lambda s, p: (there(s), 0, 0)),
                pl.BlockSpec(norm_shape, lambda s, p: (0, 0, 0)),
            ],
            scratch_shapes=[
                pltpu.VMEM((groups, cols, GROUP * bins), BF16),
                pltpu.VMEM((tile * GROUP * bins, GROUP * features), BF16),
                pltpu.VMEM((groups * seqs, tile * GROUP * bins), BF16),
                pltpu.VMEM((GROUP * features // 128, groups * seqs, 128), F32),
            ]
            + ([] if resident else [
                pltpu.VMEM(factors.shape, BF16),
                pltpu.VMEM(mix.shape, BF16),
                pltpu.SemaphoreType.DMA((2,)),
            ]),
        ),
        out_shape=[
            jax.ShapeDtypeStruct(pair_activation.shape, BF16),
            jax.ShapeDtypeStruct(norm_shape, BF16),
        ],
        input_output_aliases={parts + 8: 0} if grad else {},
        compiler_params=pltpu.CompilerParams(vmem_limit_bytes=LEAN_BYTES if resident else VMEM_BYTES),
        cost_estimate=SHORT,
        name="pair_step",
    )(part, pair_activation, *received, targets, weight_t, weight_wide, bias, factors, mix, *grad,
      *ahead)


def norm_forward(features):
    centered = features - jnp.mean(features, axis=0, keepdims=True)
    scale_inv = lax.rsqrt(jnp.mean(centered * centered, axis=0, keepdims=True) + 1e-05)
    return centered * scale_inv, scale_inv


def norm_backward(incoming, normed, scale_inv):
    first_mean = jnp.mean(incoming, axis=0, keepdims=True)
    second_mean = jnp.mean(incoming * normed, axis=0, keepdims=True)
    return scale_inv * (incoming - first_mean - normed * second_mean)


def transition_kernel(
    pieces, rows, col_devices, entry_ref, arriving_ref, mean_gain_ref, gain_ref, gate_up_t_ref,
    gate_up_ref, down_ref, down_t_ref, *refs,
):
    arrived, (out_ref, incoming) = refs[:-2], refs[-2:]
    hidden = down_ref.shape[0]
    seqs, features, positions = out_ref.shape
    groups = rows // GROUP
    row = lax.broadcasted_iota(jnp.int32, (groups, rows), 0)
    col = lax.broadcasted_iota(jnp.int32, (groups, rows), 1)
    spread = [jnp.where(col == GROUP * row + r, 1.0, 0.0).astype(BF16) for r in range(GROUP)]

    for s in range(seqs):
        for block in range(positions // rows):
            sums = []
            for which, at, count in pieces:
                at += s * count
                sums.append(
                    sum(
                        arrived[which][block * col_devices + c, at : at + count, :].astype(F32)
                        for c in range(col_devices)
                    )
                )
            field = jnp.concatenate(sums, axis=0).astype(BF16)
            incoming[s, :, block * rows : (block + 1) * rows] = sum(
                contract(field[:, r * features : (r + 1) * features], spread[r], 0, 0)
                for r in range(GROUP)
            )

    gain = gain_ref[...]
    for s in range(seqs):
        entry = entry_ref[s].astype(F32)
        normed, scale_inv = norm_forward(entry)
        normed_input = (normed * gain).astype(BF16)
        both = contract(gate_up_t_ref[...], normed_input, 1, 0)
        gate, up = both[:hidden], both[hidden:]
        sig = jax.nn.sigmoid(gate)
        silu = gate * sig
        msa_out = entry + contract(down_t_ref[...], (silu * up).astype(BF16), 1, 0)
        second_normed, second_scale = norm_forward(msa_out)
        middle = arriving_ref[s].astype(F32) + norm_backward(
            incoming[s] * mean_gain_ref[...], second_normed, second_scale
        )
        hidden_grad = contract(down_ref[...], middle.astype(BF16), 1, 0)
        gate_grad = (hidden_grad * up * sig * (1.0 + gate * (1.0 - sig))).astype(BF16)
        up_grad = (hidden_grad * silu).astype(BF16)
        normed_grad = contract(
            gate_up_ref[...], jnp.concatenate([gate_grad, up_grad], axis=0), 1, 0
        )
        out = middle + norm_backward(normed_grad * gain, normed, scale_inv)
        out_ref[s] = out.astype(BF16)


def transition(
    entry, arriving, arrived, pieces, rows, col_devices, mean_gain, gain, gate_weight, up_weight,
    down_weight,
):
    features = entry.shape[1]
    gate_up = jnp.concatenate([gate_weight, up_weight], axis=1)
    return pl.pallas_call(
        functools.partial(transition_kernel, pieces, rows, col_devices),
        out_shape=jax.ShapeDtypeStruct(entry.shape, BF16),
        scratch_shapes=[pltpu.VMEM(entry.shape, F32)],
        compiler_params=pltpu.CompilerParams(vmem_limit_bytes=VMEM_BYTES),
        name="transition",
    )(entry, arriving, mean_gain[:, None], gain[:, None], gate_up.T, gate_up, down_weight,
      down_weight.T, *arrived)


def chunk_plan(rows):
    size = max(16, rows // 4)
    return [(at, min(size, rows - at)) for at in range(0, rows, size)]


def per_device(
    pair_activation,
    target_distance_bins,
    distogram_weight,
    distogram_bias,
    outer_pair_weight,
    stored_lhs_operand,
    stored_rhs_operand,
    left_projection_weight,
    right_projection_weight,
    outer_mean_norm_gain,
    transition_norm_gain,
    gate_weight,
    up_weight,
    down_weight,
    side_stack_entry,
    arriving_stack_derivative,
):
    rows, cols, _ = pair_activation.shape
    width, bins = distogram_weight.shape
    factor_width = stored_lhs_operand.shape[1]
    features = left_projection_weight.shape[0]
    row_devices = lax.axis_size("row")
    col_devices = lax.axis_size("col")
    parts = row_devices // col_devices
    seqs = stored_lhs_operand.shape[0] * row_devices
    row_index = lax.axis_index("row").astype(jnp.int32)
    part = jnp.stack([row_index % parts, row_index // parts])
    weight_t = distogram_weight.T
    bias = distogram_bias[None, :]
    same = jnp.eye(GROUP, dtype=BF16)
    weight_wide = (same[:, None, :, None] * weight_t[None, :, None, :]).reshape(
        GROUP * bins, GROUP * width
    )

    blocks = row_devices // parts
    own = join([stored_rhs_operand, stored_lhs_operand], 1)
    others = []
    for flip in range(1, blocks):
        pairs = [((n ^ flip) * parts + h, n * parts + h) for n in range(blocks) for h in range(parts)]
        others.append(lax.ppermute(own, "row", pairs))

    across = join([own] + others, 0)
    shifted = [across]
    for shift in range(1, parts):
        pairs = [
            (n * parts + (h + shift) % parts, n * parts + h)
            for n in range(blocks) for h in range(parts)
        ]
        shifted.append(lax.ppermute(across, "row", pairs))
    factors = jnp.concatenate(shifted).reshape(seqs, 2 * factor_width, cols)
    factors = factors.swapaxes(0, 1).reshape(2 * factor_width * seqs, cols)

    outer_weight = outer_pair_weight.astype(F32).reshape(factor_width, factor_width, width)
    by_bin = jnp.einsum(
        "pb,cep->bce", distogram_weight.astype(F32), outer_weight, precision=lax.Precision.HIGHEST
    )
    mix_right = jnp.einsum(
        "mc,bce->ebm", left_projection_weight.astype(F32), by_bin, precision=lax.Precision.HIGHEST
    )
    mix_left = jnp.einsum(
        "me,bce->cbm", right_projection_weight.astype(F32), by_bin, precision=lax.Precision.HIGHEST
    )
    mix = (jnp.concatenate([mix_right, mix_left], axis=0) / seqs).astype(BF16)
    mix = jnp.concatenate([mix, mix], axis=2)

    devices = row_devices * col_devices
    exchange = functools.partial(
        lax.all_to_all, axis_name=AXES, split_axis=0, concat_axis=0, tiled=True
    )
    chunks = chunk_plan(rows)
    count = len(chunks)
    leg_pairs = first_leg(col_devices, parts)
    first, logits, sent, relayed, received = [], [], [], [], []
    norm_parts, arrived, grad = [], [], []
    for n in range(count + 2):
        while len(first) < min(2, count):
            first.append(
                mirror_logits(
                    part, pair_activation, weight_t, bias, *chunks[len(first)], parts, first[-1:]
                )
            )
        for m in range(len(logits), min(count, n + 2)):
            before = others if m < 2 else relayed[m - 2] + sum(received[: m - 2][-1:], [])
            logits.append(tie(first[m], before))
            sent.append(lax.ppermute(logits[m], AXES, leg_pairs))
        while len(first) < count:
            first.append(
                mirror_logits(
                    part, pair_activation, weight_t, bias, *chunks[len(first)], parts,
                    logits[-1:] if len(first) == 2 else first[-1:],
                )
            )
        if n >= min(2, count):
            now = n - min(2, count)
            if now < count:
                ahead = logits[n : n + 1] + [x for arrays in relayed[now + 1 :] for x in arrays]
                if now == count - 1 and now > 0:
                    early = join(norm_parts, 1, received[now])
                    arrived.append(exchange(early))
                    ahead = [early]
                *grad, norm_part = pair_step(
                    part, pair_activation, received[now], target_distance_bins, weight_t,
                    weight_wide, bias, factors, mix, grad, chunks[now][0], seqs, devices,
                    row_devices, ahead, now < count - 1,
                )
                norm_parts.append(norm_part)
        if n < count:
            before = [[across, mix, weight_wide], [factors]][n] if n < 2 else [norm_parts[n - 2]]
            before = before + (first[2:] if n == 0 else logits[n + 1 : n + 2])
            relayed.append(list(split(sent[n], before)))
            received.append(
                [
                    lax.ppermute(piece, AXES, second_leg(col_devices, parts, shift))
                    for shift, piece in enumerate(relayed[n])
                ]
            )
    final = norm_parts[-1]
    if arrived:
        final, arrived[0] = lax.optimization_barrier((final, arrived[0]))
    arrived.append(exchange(final))
    pieces = []
    for n, part_sums in enumerate(norm_parts):
        last = n == len(chunks) - 1 and n > 0
        at = 0 if last else sum(x.shape[1] for x in norm_parts[:n])
        pieces.append((int(last), at, chunks[n][1] // GROUP))
    alignment_gradient = transition(
        side_stack_entry, arriving_stack_derivative, arrived, pieces, rows, col_devices,
        outer_mean_norm_gain, transition_norm_gain, gate_weight, up_weight, down_weight,
    )
    return grad[0], alignment_gradient


def solution(mesh):
    return jax.shard_map(
        per_device,
        mesh=mesh,
        in_specs=(
            P("row", "col", None),
            P("row", "col"),
            P(),
            P(),
            P(),
            P("row", None, "col"),
            P("row", None, "col"),
            P(),
            P(),
            P(),
            P(),
            P(),
            P(),
            P(),
            P(AXES, None, None),
            P(AXES, None, None),
        ),
        out_specs=(P("row", "col", None), P(AXES, None, None)),
        check_vma=False,
    )
```

```python
import functools

import jax
import jax.numpy as jnp
from jax import lax
from jax.experimental import pallas as pl
from jax.experimental.pallas import tpu as pltpu
from jax.sharding import PartitionSpec as P

BF16, F32 = jnp.bfloat16, jnp.float32
VMEM_BYTES = 56 * 1024 * 1024
LEAN_BYTES = 32 * 1024 * 1024
AXES = ("row", "col")
GROUP = 4
SHORT = pl.CostEstimate(flops=0, bytes_accessed=0, transcendentals=0)
LONG = pl.CostEstimate(flops=16 * 10**9, bytes_accessed=40 * 10**6, transcendentals=0)


def contract(lhs, rhs, lhs_dim, rhs_dim):
    return lax.dot_general(
        lhs, rhs, (((lhs_dim,), (rhs_dim,)), ((), ())), preferred_element_type=F32
    )


def relay(block, z, blocks):
    if blocks % 4:
        return z, block
    low_block = ((1 - (block & 1)) << 1) | (z & 1)
    low_z = (z & 2) | ((block >> 1) & 1)
    return (z >> 2 << 2) | low_block, (block >> 2 << 2) | low_z


def first_leg(blocks, parts):
    pairs = []
    for block in range(blocks):
        for z in range(blocks):
            to_block, to_z = relay(block, z, blocks)
            for h in range(parts):
                pairs.append(
                    ((block * parts + h) * blocks + z, (to_block * parts + h) * blocks + to_z)
                )
    return pairs


def second_leg(blocks, parts, shift):
    pairs = []
    for block in range(blocks):
        for z in range(blocks):
            via_block, via_z = relay(block, z, blocks)
            for h in range(parts):
                pairs.append(
                    (
                        (via_block * parts + h) * blocks + via_z,
                        (z * parts + (h + shift) % parts) * blocks + block,
                    )
                )
    return pairs


def as_column(row):
    n = row.shape[1]
    across = lax.broadcasted_iota(jnp.int32, (n, n), 0)
    along = lax.broadcasted_iota(jnp.int32, (n, n), 1)
    return jnp.sum(jnp.where(across == along, row, 0.0), axis=1, keepdims=True)


def mirror_logits_kernel(part_ref, pair_ref, weight_ref, bias_ref, *refs):
    out_ref, widened = refs[-2:]
    own_rows, step_cols, width = pair_ref.shape
    widened[...] = pair_ref[...].astype(F32).reshape(own_rows * step_cols, width)
    weight = weight_ref[...]
    bias = as_column(bias_ref[...])
    for j in range(step_cols):
        column = widened[pl.ds(j, own_rows, stride=step_cols), :].astype(BF16)
        out_ref[0, j] = (contract(weight, column, 1, 1) + bias).astype(BF16)


def mirror_logits(part, pair_activation, weight_t, bias, first_row, chunk_rows, parts, ahead):
    rows, cols, width = pair_activation.shape
    bins = weight_t.shape[0]
    step = min(16, chunk_rows)
    steps = chunk_rows // step

    def block(s, part_ref):
        half = lax.rem(part_ref[0] + s // steps, parts)
        return (0, half * (rows // step) + first_row // step + lax.rem(s, steps), 0)

    return pl.pallas_call(
        mirror_logits_kernel,
        grid_spec=pltpu.PrefetchScalarGridSpec(
            num_scalar_prefetch=1,
            grid=(parts * steps,),
            in_specs=[
                pl.BlockSpec((rows, step, width), block),
                pl.BlockSpec((bins, width), lambda s, p: (0, 0)),
                pl.BlockSpec((1, bins), lambda s, p: (0, 0)),
            ]
            + [pl.BlockSpec(memory_space=pl.ANY)] * len(ahead),
            out_specs=pl.BlockSpec(
                (1, step, bins, rows), lambda s, p: (s // steps, lax.rem(s, steps), 0, 0)
            ),
            scratch_shapes=[pltpu.VMEM((rows * step, width), F32)],
        ),
        out_shape=jax.ShapeDtypeStruct((parts, chunk_rows, bins, rows), BF16),
        compiler_params=pltpu.CompilerParams(vmem_limit_bytes=VMEM_BYTES),
        cost_estimate=SHORT,
        name="mirror_logits",
    )(part, pair_activation, weight_t, bias, *ahead)


def own_logits_kernel(pair_ref, weight_ref, bias_ref, *refs):
    out_ref = refs[-1]
    weight = weight_ref[...]
    bias = as_column(bias_ref[...])
    for i in range(pair_ref.shape[0]):
        out_ref[i] = (contract(weight, pair_ref[i], 1, 1) + bias).astype(BF16)


def own_logits(pair_activation, weight_t, bias, first_row, chunk_rows, ahead):
    rows, cols, width = pair_activation.shape
    bins = weight_t.shape[0]
    step = min(8, chunk_rows)
    return pl.pallas_call(
        own_logits_kernel,
        grid=(chunk_rows // step,),
        in_specs=[
            pl.BlockSpec((step, cols, width), lambda s: (first_row // step + s, 0, 0)),
            pl.BlockSpec((bins, width), lambda s: (0, 0)),
            pl.BlockSpec((1, bins), lambda s: (0, 0)),
        ]
        + [pl.BlockSpec(memory_space=pl.ANY)] * len(ahead),
        out_specs=pl.BlockSpec((step, bins, cols), lambda s: (s, 0, 0)),
        out_shape=jax.ShapeDtypeStruct((chunk_rows, bins, cols), BF16),
        compiler_params=pltpu.CompilerParams(vmem_limit_bytes=LEAN_BYTES),
        cost_estimate=SHORT,
        name="own_logits",
    )(pair_activation, weight_t, bias, *ahead)


def tie_kernel(*refs):
    pass


def tie(array, ahead):
    anywhere = pl.BlockSpec(memory_space=pl.ANY)
    return pl.pallas_call(
        tie_kernel,
        in_specs=[anywhere] * (1 + len(ahead)),
        out_specs=anywhere,
        out_shape=jax.ShapeDtypeStruct(array.shape, array.dtype),
        input_output_aliases={0: 0},
        compiler_params=pltpu.CompilerParams(vmem_limit_bytes=LEAN_BYTES),
        name="tie",
    )(array, *ahead)


def split_kernel(in_ref, *refs):
    for n, out_ref in enumerate(refs[-in_ref.shape[0] :]):
        out_ref[...] = in_ref[n]


def split(array, ahead):
    count, rows, *rest = array.shape
    step = min(16, rows)
    return pl.pallas_call(
        split_kernel,
        grid=(rows // step,),
        in_specs=[pl.BlockSpec((count, step, *rest), lambda s: (0, s, 0, 0))]
        + [pl.BlockSpec(memory_space=pl.ANY)] * len(ahead),
        out_specs=[pl.BlockSpec((step, *rest), lambda s: (s, 0, 0))] * count,
        out_shape=[jax.ShapeDtypeStruct(array.shape[1:], array.dtype)] * count,
        compiler_params=pltpu.CompilerParams(vmem_limit_bytes=LEAN_BYTES),
        name="split",
    )(array, *ahead)


def join_kernel(axis, count, *refs):
    out_ref = refs[-1]
    at = 0
    for ref in refs[:count]:
        end = at + ref.shape[axis]
        if axis:
            out_ref[:, at:end] = ref[...]
        else:
            out_ref[at:end] = ref[...]
        at = end


def join(arrays, axis, ahead=()):
    shape = list(arrays[0].shape)
    shape[axis] = sum(array.shape[axis] for array in arrays)
    vmem = pl.BlockSpec(memory_space=pltpu.VMEM)
    return pl.pallas_call(
        functools.partial(join_kernel, axis, len(arrays)),
        in_specs=[vmem] * len(arrays) + [pl.BlockSpec(memory_space=pl.ANY)] * len(ahead),
        out_specs=vmem,
        out_shape=jax.ShapeDtypeStruct(shape, BF16),
        compiler_params=pltpu.CompilerParams(vmem_limit_bytes=LEAN_BYTES),
        name="join",
    )(*arrays, *ahead)


def pair_kernel(parts, slots, front, tile, resident, part_ref, own_ref, *refs):
    received = refs[:parts]
    target_ref, weight_wide_ref, factors, mix = refs[parts : parts + 4]
    if resident:
        grad_ref, norm_ref, slopes, mix_wide, mixed, total = refs[-6:]
        copies = []
    else:
        grad_ref, norm_ref, slopes, mix_wide, mixed, total, factor_copy, mix_copy, sems = refs[-9:]
        copies = [
            pltpu.make_async_copy(factors, factor_copy, sems.at[0]),
            pltpu.make_async_copy(mix, mix_copy, sems.at[1]),
        ]
        factors, mix = factor_copy, mix_copy
    step = pl.program_id(0)
    step_rows, cols, width = grad_ref.shape
    bins = own_ref.shape[1]
    groups = slopes.shape[0]
    step_groups = step_rows // GROUP
    features = total.shape[0] * total.shape[2] // GROUP
    devices, device_rows, _ = norm_ref.shape
    device_seqs = device_rows // groups
    seqs = devices * device_seqs
    xs = mix.shape[0]
    base = step * step_rows if resident else 0

    @pl.when(step == 0)
    def _():
        for copy in copies:
            copy.start()
        total[...] = jnp.zeros_like(total)
        mix_wide[...] = jnp.zeros_like(mix_wide)

    @pl.when(step < front)
    def _():
        h = part_ref[0]
        levels = lax.broadcasted_iota(jnp.int32, (bins, cols), 0)
        for g in range(step_groups):
            group = []
            for r in range(GROUP):
                i = g * GROUP + r
                own = own_ref[base + i].astype(F32)
                halves = []
                for u in range(parts):
                    half = received[0][base + i]
                    for shift in range(1, parts):
                        half = jnp.where(
                            lax.rem(h + parts - u, parts) == shift, received[shift][base + i], half
                        )
                    halves.append(half)
                symmetric = own + jnp.concatenate(halves, axis=1).astype(F32)
                top = jnp.max(symmetric, axis=0, keepdims=True)
                raised = jnp.exp(symmetric - top)
                scale = 2.0 / jnp.sum(raised, axis=0, keepdims=True)
                hit = jnp.where(levels == target_ref[i : i + 1, :], 2.0, 0.0)
                group.append((raised * scale - hit).astype(BF16))
            slope = jnp.concatenate(group, axis=0).T
            slopes[step * step_groups + g] = slope
            out = contract(slope, weight_wide_ref[...], 1, 0).astype(BF16)
            for r in range(GROUP):
                grad_ref[g * GROUP + r] = out[:, r * width : (r + 1) * width]

    @pl.when(step == front)
    def _():
        for copy in copies:
            copy.wait()
        half_groups = max(1, groups // 2)

        def add_tile(t, carry):
            for x in range(tile):
                for r in range(GROUP):
                    rows = pl.ds((x * GROUP + r) * bins, bins)
                    at = r * features
                    mix_wide[rows, at : at + features] = (
                        mix[t * tile + x, :, at % 128 : at % 128 + features]
                    )
            factor = factors[pl.ds(pl.multiple_of(t * tile * seqs, tile * seqs), tile * seqs), :]
            for g in range(groups):
                spread = contract(factor, slopes[g], 1, 0).astype(BF16)
                for x in range(tile):
                    mixed[g * seqs : (g + 1) * seqs, x * GROUP * bins : (x + 1) * GROUP * bins] = (
                        spread[x * seqs : (x + 1) * seqs, :]
                    )
            for g in range(0, groups, half_groups):
                rows = slice(g * seqs, (g + half_groups) * seqs)
                term = contract(mixed[rows, :], mix_wide[...], 1, 0)
                for c in range(total.shape[0]):
                    total[c, rows, :] += term[:, c * 128 : (c + 1) * 128]
            return carry

        lax.fori_loop(0, xs // tile, add_tile, 0)
        slot_seqs = seqs // slots
        for s in range(seqs):
            slot, rest = divmod(s, slot_seqs)
            device, k = divmod(rest, device_seqs)
            other, pair = divmod(slot, slots // parts)
            block = part_ref[1] ^ pair
            device += (block * parts + lax.rem(part_ref[0] + other, parts)) * (devices // slots)
            for c in range(total.shape[0]):
                norm_ref[device, k * groups : (k + 1) * groups, c * 128 : (c + 1) * 128] = (
                    total[c, pl.ds(s, groups, stride=seqs), :].astype(BF16)
                )


def pair_step(
    part, shape, own, received, targets, weight_wide, factors, mix, grad,
    first_row, seqs, devices, slots, ahead, resident,
):
    _, cols, width = shape
    bins = own.shape[1]
    features = mix.shape[2] // 2
    parts = len(received)
    chunk_rows = received[0].shape[0]
    step_rows = min(16, chunk_rows)
    groups = chunk_rows // GROUP
    xs = factors.shape[0] // seqs
    tile = max(1, min(8, 512 // seqs))
    front = chunk_rows // step_rows
    near = lambda s: jnp.minimum(s, front - 1)
    anywhere = pl.BlockSpec(memory_space=pl.ANY)
    if resident:
        mine = held = moved = pl.BlockSpec(memory_space=pltpu.VMEM)
    else:
        held = pl.BlockSpec((step_rows, bins, cols // parts), lambda s, p: (near(s), 0, 0))
        mine = pl.BlockSpec((step_rows, bins, cols), lambda s, p: (near(s), 0, 0))
        moved = anywhere
    there = lambda s: first_row // step_rows + jnp.minimum(s, front - 1)
    const2 = lambda s, p: (0, 0)
    norm_shape = (devices, seqs // devices * groups, GROUP * features)
    return pl.pallas_call(
        functools.partial(pair_kernel, parts, slots, front, tile, resident),
        grid_spec=pltpu.PrefetchScalarGridSpec(
            num_scalar_prefetch=1,
            grid=(front + 1,),
            in_specs=[mine]
            + [held] * parts
            + [
                pl.BlockSpec((step_rows, cols), lambda s, p: (there(s), 0)),
                pl.BlockSpec((GROUP * bins, GROUP * width), const2),
            ]
            + [moved] * 2
            + [pl.BlockSpec(memory_space=pltpu.HBM)] * len(grad)
            + [anywhere] * len(ahead),
            out_specs=[
                pl.BlockSpec((step_rows, cols, width), lambda s, p: (there(s), 0, 0)),
                pl.BlockSpec(norm_shape, lambda s, p: (0, 0, 0)),
            ],
            scratch_shapes=[
                pltpu.VMEM((groups, cols, GROUP * bins), BF16),
                pltpu.VMEM((tile * GROUP * bins, GROUP * features), BF16),
                pltpu.VMEM((groups * seqs, tile * GROUP * bins), BF16),
                pltpu.VMEM((GROUP * features // 128, groups * seqs, 128), F32),
            ]
            + ([] if resident else [
                pltpu.VMEM(factors.shape, BF16),
                pltpu.VMEM(mix.shape, BF16),
                pltpu.SemaphoreType.DMA((2,)),
            ]),
        ),
        out_shape=[
            jax.ShapeDtypeStruct(shape, BF16),
            jax.ShapeDtypeStruct(norm_shape, BF16),
        ],
        input_output_aliases={parts + 6: 0} if grad else {},
        compiler_params=pltpu.CompilerParams(vmem_limit_bytes=LEAN_BYTES if resident else VMEM_BYTES),
        cost_estimate=LONG,
        name="pair_step",
    )(part, own, *received, targets, weight_wide, factors, mix, *grad, *ahead)


def norm_forward(features):
    centered = features - jnp.mean(features, axis=0, keepdims=True)
    scale_inv = lax.rsqrt(jnp.mean(centered * centered, axis=0, keepdims=True) + 1e-05)
    return centered * scale_inv, scale_inv


def norm_backward(incoming, normed, scale_inv):
    first_mean = jnp.mean(incoming, axis=0, keepdims=True)
    second_mean = jnp.mean(incoming * normed, axis=0, keepdims=True)
    return scale_inv * (incoming - first_mean - normed * second_mean)


def transition_kernel(
    pieces, rows, col_devices, entry_ref, arriving_ref, mean_gain_ref, gain_ref, gate_up_t_ref,
    gate_up_ref, down_ref, down_t_ref, *refs,
):
    arrived, (out_ref, incoming) = refs[:-2], refs[-2:]
    hidden = down_ref.shape[0]
    seqs, features, positions = out_ref.shape
    groups = rows // GROUP
    row = lax.broadcasted_iota(jnp.int32, (groups, rows), 0)
    col = lax.broadcasted_iota(jnp.int32, (groups, rows), 1)
    spread = [jnp.where(col == GROUP * row + r, 1.0, 0.0).astype(BF16) for r in range(GROUP)]

    for s in range(seqs):
        for block in range(positions // rows):
            sums = []
            for which, at, count in pieces:
                at += s * count
                sums.append(
                    sum(
                        arrived[which][block * col_devices + c, at : at + count, :].astype(F32)
                        for c in range(col_devices)
                    )
                )
            field = jnp.concatenate(sums, axis=0).astype(BF16)
            incoming[s, :, block * rows : (block + 1) * rows] = sum(
                contract(field[:, r * features : (r + 1) * features], spread[r], 0, 0)
                for r in range(GROUP)
            )

    gain = gain_ref[...]
    for s in range(seqs):
        entry = entry_ref[s].astype(F32)
        normed, scale_inv = norm_forward(entry)
        normed_input = (normed * gain).astype(BF16)
        both = contract(gate_up_t_ref[...], normed_input, 1, 0)
        gate, up = both[:hidden], both[hidden:]
        sig = jax.nn.sigmoid(gate)
        silu = gate * sig
        msa_out = entry + contract(down_t_ref[...], (silu * up).astype(BF16), 1, 0)
        second_normed, second_scale = norm_forward(msa_out)
        middle = arriving_ref[s].astype(F32) + norm_backward(
            incoming[s] * mean_gain_ref[...], second_normed, second_scale
        )
        hidden_grad = contract(down_ref[...], middle.astype(BF16), 1, 0)
        gate_grad = (hidden_grad * up * sig * (1.0 + gate * (1.0 - sig))).astype(BF16)
        up_grad = (hidden_grad * silu).astype(BF16)
        normed_grad = contract(
            gate_up_ref[...], jnp.concatenate([gate_grad, up_grad], axis=0), 1, 0
        )
        out = middle + norm_backward(normed_grad * gain, normed, scale_inv)
        out_ref[s] = out.astype(BF16)


def transition(
    entry, arriving, arrived, pieces, rows, col_devices, mean_gain, gain, gate_weight, up_weight,
    down_weight,
):
    features = entry.shape[1]
    gate_up = jnp.concatenate([gate_weight, up_weight], axis=1)
    return pl.pallas_call(
        functools.partial(transition_kernel, pieces, rows, col_devices),
        out_shape=jax.ShapeDtypeStruct(entry.shape, BF16),
        scratch_shapes=[pltpu.VMEM(entry.shape, F32)],
        compiler_params=pltpu.CompilerParams(vmem_limit_bytes=VMEM_BYTES),
        name="transition",
    )(entry, arriving, mean_gain[:, None], gain[:, None], gate_up.T, gate_up, down_weight,
      down_weight.T, *arrived)


def chunk_plan(rows):
    size = max(16, rows // 4)
    return [(at, min(size, rows - at)) for at in range(0, rows, size)]


def per_device(
    pair_activation,
    target_distance_bins,
    distogram_weight,
    distogram_bias,
    outer_pair_weight,
    stored_lhs_operand,
    stored_rhs_operand,
    left_projection_weight,
    right_projection_weight,
    outer_mean_norm_gain,
    transition_norm_gain,
    gate_weight,
    up_weight,
    down_weight,
    side_stack_entry,
    arriving_stack_derivative,
):
    rows, cols, _ = pair_activation.shape
    width, bins = distogram_weight.shape
    factor_width = stored_lhs_operand.shape[1]
    features = left_projection_weight.shape[0]
    row_devices = lax.axis_size("row")
    col_devices = lax.axis_size("col")
    parts = row_devices // col_devices
    seqs = stored_lhs_operand.shape[0] * row_devices
    row_index = lax.axis_index("row").astype(jnp.int32)
    part = jnp.stack([row_index % parts, row_index // parts])
    weight_t = distogram_weight.T
    bias = distogram_bias[None, :]
    same = jnp.eye(GROUP, dtype=BF16)
    weight_wide = (same[:, None, :, None] * weight_t[None, :, None, :]).reshape(
        GROUP * bins, GROUP * width
    )

    blocks = row_devices // parts
    own = join([stored_rhs_operand, stored_lhs_operand], 1)
    others = []
    for flip in range(1, blocks):
        pairs = [((n ^ flip) * parts + h, n * parts + h) for n in range(blocks) for h in range(parts)]
        others.append(lax.ppermute(own, "row", pairs))

    across = join([own] + others, 0)
    shifted = [across]
    for shift in range(1, parts):
        pairs = [
            (n * parts + (h + shift) % parts, n * parts + h)
            for n in range(blocks) for h in range(parts)
        ]
        shifted.append(lax.ppermute(across, "row", pairs))
    factors = jnp.concatenate(shifted).reshape(seqs, 2 * factor_width, cols)
    factors = factors.swapaxes(0, 1).reshape(2 * factor_width * seqs, cols)

    outer_weight = outer_pair_weight.astype(F32).reshape(factor_width, factor_width, width)
    by_bin = jnp.einsum(
        "pb,cep->bce", distogram_weight.astype(F32), outer_weight, precision=lax.Precision.HIGHEST
    )
    mix_right = jnp.einsum(
        "mc,bce->ebm", left_projection_weight.astype(F32), by_bin, precision=lax.Precision.HIGHEST
    )
    mix_left = jnp.einsum(
        "me,bce->cbm", right_projection_weight.astype(F32), by_bin, precision=lax.Precision.HIGHEST
    )
    mix = (jnp.concatenate([mix_right, mix_left], axis=0) / seqs).astype(BF16)
    mix = jnp.concatenate([mix, mix], axis=2)

    devices = row_devices * col_devices
    exchange = functools.partial(
        lax.all_to_all, axis_name=AXES, split_axis=0, concat_axis=0, tiled=True
    )
    chunks = chunk_plan(rows)
    count = len(chunks)
    leg_pairs = first_leg(col_devices, parts)
    first, logits, sent, relayed, received = [], [], [], [], []
    owns, norm_parts, arrived, grad = [], [], [], []
    for n in range(count + 2):
        while len(first) < min(2, count):
            first.append(
                mirror_logits(
                    part, pair_activation, weight_t, bias, *chunks[len(first)], parts, first[-1:]
                )
            )
        for m in range(len(logits), min(count, n + 2)):
            before = others if m < 2 else relayed[m - 2] + sum(received[: m - 2][-1:], [])
            logits.append(tie(first[m], before))
            sent.append(lax.ppermute(logits[m], AXES, leg_pairs))
        while len(first) < count:
            first.append(
                mirror_logits(
                    part, pair_activation, weight_t, bias, *chunks[len(first)], parts,
                    logits[-1:] if len(first) == 2 else first[-1:],
                )
            )
        if n >= min(2, count):
            now = n - min(2, count)
            if now < count:
                ahead = logits[n : n + 1] + [x for arrays in relayed[now + 1 :] for x in arrays]
                if now == count - 1 and now > 0:
                    early = join(norm_parts, 1, received[now])
                    arrived.append(exchange(early))
                    ahead = [early]
                *grad, norm_part = pair_step(
                    part, pair_activation.shape, owns[now], received[now], target_distance_bins,
                    weight_wide, factors, mix, grad, chunks[now][0], seqs, devices, row_devices,
                    ahead, now < count - 1,
                )
                norm_parts.append(norm_part)
        if n < count:
            before = [[across, mix, weight_wide], [factors]][n] if n < 2 else [norm_parts[n - 2]]
            if n == 0:
                before = before + first[2:]
            if n < 2:
                for chunk in chunks[2 * n :][: 2 if n == 0 else count]:
                    owns.append(
                        own_logits(
                            pair_activation, weight_t, bias, *chunk,
                            owns[-1:] + (first[-1:] if n == 0 else relayed[0]),
                        )
                    )
                before = before + owns[2 * n :]
            relayed.append(list(split(sent[n], before)))
            received.append(
                [
                    lax.ppermute(piece, AXES, second_leg(col_devices, parts, shift))
                    for shift, piece in enumerate(relayed[n])
                ]
            )
    final = norm_parts[-1]
    if arrived:
        final, arrived[0] = lax.optimization_barrier((final, arrived[0]))
    arrived.append(exchange(final))
    pieces = []
    for n, part_sums in enumerate(norm_parts):
        last = n == len(chunks) - 1 and n > 0
        at = 0 if last else sum(x.shape[1] for x in norm_parts[:n])
        pieces.append((int(last), at, chunks[n][1] // GROUP))
    alignment_gradient = transition(
        side_stack_entry, arriving_stack_derivative, arrived, pieces, rows, col_devices,
        outer_mean_norm_gain, transition_norm_gain, gate_weight, up_weight, down_weight,
    )
    return grad[0], alignment_gradient


def solution(mesh):
    return jax.shard_map(
        per_device,
        mesh=mesh,
        in_specs=(
            P("row", "col", None),
            P("row", "col"),
            P(),
            P(),
            P(),
            P("row", None, "col"),
            P("row", None, "col"),
            P(),
            P(),
            P(),
            P(),
            P(),
            P(),
            P(),
            P(AXES, None, None),
            P(AXES, None, None),
        ),
        out_specs=(P("row", "col", None), P(AXES, None, None)),
        check_vma=False,
    )
```

```python
import functools

import jax
import jax.numpy as jnp
from jax import lax
from jax.experimental import pallas as pl
from jax.experimental.pallas import tpu as pltpu
from jax.sharding import PartitionSpec as P

BF16, F32 = jnp.bfloat16, jnp.float32
VMEM_BYTES = 56 * 1024 * 1024
LEAN_BYTES = 32 * 1024 * 1024
AXES = ("row", "col")
GROUP = 4
SHORT = pl.CostEstimate(flops=0, bytes_accessed=0, transcendentals=0)
LONG = pl.CostEstimate(flops=16 * 10**9, bytes_accessed=40 * 10**6, transcendentals=0)


def contract(lhs, rhs, lhs_dim, rhs_dim):
    return lax.dot_general(
        lhs, rhs, (((lhs_dim,), (rhs_dim,)), ((), ())), preferred_element_type=F32
    )


def relay(block, z, blocks):
    if blocks % 4:
        return z, block
    low_block = ((1 - (block & 1)) << 1) | (z & 1)
    low_z = (z & 2) | ((block >> 1) & 1)
    return (z >> 2 << 2) | low_block, (block >> 2 << 2) | low_z


def first_leg(blocks, parts):
    pairs = []
    for block in range(blocks):
        for z in range(blocks):
            to_block, to_z = relay(block, z, blocks)
            for h in range(parts):
                pairs.append(
                    ((block * parts + h) * blocks + z, (to_block * parts + h) * blocks + to_z)
                )
    return pairs


def second_leg(blocks, parts, shift):
    pairs = []
    for block in range(blocks):
        for z in range(blocks):
            via_block, via_z = relay(block, z, blocks)
            for h in range(parts):
                pairs.append(
                    (
                        (via_block * parts + h) * blocks + via_z,
                        (z * parts + (h + shift) % parts) * blocks + block,
                    )
                )
    return pairs


def as_column(row):
    n = row.shape[1]
    across = lax.broadcasted_iota(jnp.int32, (n, n), 0)
    along = lax.broadcasted_iota(jnp.int32, (n, n), 1)
    return jnp.sum(jnp.where(across == along, row, 0.0), axis=1, keepdims=True)


def mirror_logits_kernel(part_ref, pair_ref, weight_ref, bias_ref, *refs):
    out_ref, widened = refs[-2:]
    own_rows, step_cols, width = pair_ref.shape
    widened[...] = pair_ref[...].astype(F32).reshape(own_rows * step_cols, width)
    weight = weight_ref[...]
    bias = as_column(bias_ref[...])
    for j in range(step_cols):
        column = widened[pl.ds(j, own_rows, stride=step_cols), :].astype(BF16)
        out_ref[0, j] = (contract(weight, column, 1, 1) + bias).astype(BF16)


def mirror_logits(part, pair_activation, weight_t, bias, first_row, chunk_rows, parts, ahead):
    rows, cols, width = pair_activation.shape
    bins = weight_t.shape[0]
    step = min(16, chunk_rows)
    steps = chunk_rows // step

    def block(s, part_ref):
        half = lax.rem(part_ref[0] + s // steps, parts)
        return (0, half * (rows // step) + first_row // step + lax.rem(s, steps), 0)

    return pl.pallas_call(
        mirror_logits_kernel,
        grid_spec=pltpu.PrefetchScalarGridSpec(
            num_scalar_prefetch=1,
            grid=(parts * steps,),
            in_specs=[
                pl.BlockSpec((rows, step, width), block),
                pl.BlockSpec((bins, width), lambda s, p: (0, 0)),
                pl.BlockSpec((1, bins), lambda s, p: (0, 0)),
            ]
            + [pl.BlockSpec(memory_space=pl.ANY)] * len(ahead),
            out_specs=pl.BlockSpec(
                (1, step, bins, rows), lambda s, p: (s // steps, lax.rem(s, steps), 0, 0)
            ),
            scratch_shapes=[pltpu.VMEM((rows * step, width), F32)],
        ),
        out_shape=jax.ShapeDtypeStruct((parts, chunk_rows, bins, rows), BF16),
        compiler_params=pltpu.CompilerParams(vmem_limit_bytes=VMEM_BYTES),
        cost_estimate=SHORT,
        name="mirror_logits",
    )(part, pair_activation, weight_t, bias, *ahead)


def own_logits_kernel(pair_ref, weight_ref, bias_ref, *refs):
    out_ref = refs[-1]
    weight = weight_ref[...]
    bias = as_column(bias_ref[...])
    for i in range(pair_ref.shape[0]):
        out_ref[i] = (contract(weight, pair_ref[i], 1, 1) + bias).astype(BF16)


def own_logits(pair_activation, weight_t, bias, first_row, chunk_rows, ahead):
    rows, cols, width = pair_activation.shape
    bins = weight_t.shape[0]
    step = min(8, chunk_rows)
    return pl.pallas_call(
        own_logits_kernel,
        grid=(chunk_rows // step,),
        in_specs=[
            pl.BlockSpec((step, cols, width), lambda s: (first_row // step + s, 0, 0)),
            pl.BlockSpec((bins, width), lambda s: (0, 0)),
            pl.BlockSpec((1, bins), lambda s: (0, 0)),
        ]
        + [pl.BlockSpec(memory_space=pl.ANY)] * len(ahead),
        out_specs=pl.BlockSpec((step, bins, cols), lambda s: (s, 0, 0)),
        out_shape=jax.ShapeDtypeStruct((chunk_rows, bins, cols), BF16),
        compiler_params=pltpu.CompilerParams(vmem_limit_bytes=LEAN_BYTES),
        cost_estimate=SHORT,
        name="own_logits",
    )(pair_activation, weight_t, bias, *ahead)


def tie_kernel(*refs):
    pass


def tie(array, ahead):
    anywhere = pl.BlockSpec(memory_space=pl.ANY)
    return pl.pallas_call(
        tie_kernel,
        in_specs=[anywhere] * (1 + len(ahead)),
        out_specs=anywhere,
        out_shape=jax.ShapeDtypeStruct(array.shape, array.dtype),
        input_output_aliases={0: 0},
        compiler_params=pltpu.CompilerParams(vmem_limit_bytes=LEAN_BYTES),
        name="tie",
    )(array, *ahead)


def split_kernel(in_ref, *refs):
    for n, out_ref in enumerate(refs[-in_ref.shape[0] :]):
        out_ref[...] = in_ref[n]


def split(array, ahead):
    count, rows, *rest = array.shape
    step = min(16, rows)
    return pl.pallas_call(
        split_kernel,
        grid=(rows // step,),
        in_specs=[pl.BlockSpec((count, step, *rest), lambda s: (0, s, 0, 0))]
        + [pl.BlockSpec(memory_space=pl.ANY)] * len(ahead),
        out_specs=[pl.BlockSpec((step, *rest), lambda s: (s, 0, 0))] * count,
        out_shape=[jax.ShapeDtypeStruct(array.shape[1:], array.dtype)] * count,
        compiler_params=pltpu.CompilerParams(vmem_limit_bytes=LEAN_BYTES),
        name="split",
    )(array, *ahead)


def join_kernel(axis, count, *refs):
    out_ref = refs[-1]
    at = 0
    for ref in refs[:count]:
        end = at + ref.shape[axis]
        if axis:
            out_ref[:, at:end] = ref[...]
        else:
            out_ref[at:end] = ref[...]
        at = end


def join(arrays, axis, ahead=()):
    shape = list(arrays[0].shape)
    shape[axis] = sum(array.shape[axis] for array in arrays)
    vmem = pl.BlockSpec(memory_space=pltpu.VMEM)
    return pl.pallas_call(
        functools.partial(join_kernel, axis, len(arrays)),
        in_specs=[vmem] * len(arrays) + [pl.BlockSpec(memory_space=pl.ANY)] * len(ahead),
        out_specs=vmem,
        out_shape=jax.ShapeDtypeStruct(shape, BF16),
        compiler_params=pltpu.CompilerParams(vmem_limit_bytes=LEAN_BYTES),
        name="join",
    )(*arrays, *ahead)


def pair_kernel(parts, slots, front, tile, resident, part_ref, own_ref, *refs):
    received = refs[:parts]
    target_ref, weight_wide_ref, factors, mix = refs[parts : parts + 4]
    if resident:
        grad_ref, norm_ref, slopes, mix_wide, mixed, total = refs[-6:]
        copies = []
    else:
        grad_ref, norm_ref, slopes, mix_wide, mixed, total, factor_copy, mix_copy, sems = refs[-9:]
        copies = [
            pltpu.make_async_copy(factors, factor_copy, sems.at[0]),
            pltpu.make_async_copy(mix, mix_copy, sems.at[1]),
        ]
        factors, mix = factor_copy, mix_copy
    step = pl.program_id(0)
    step_rows, cols, width = grad_ref.shape
    bins = own_ref.shape[1]
    groups = slopes.shape[0]
    step_groups = step_rows // GROUP
    features = total.shape[0] * total.shape[2] // GROUP
    devices, device_rows, _ = norm_ref.shape
    device_seqs = device_rows // groups
    seqs = devices * device_seqs
    xs = mix.shape[0]
    base = step * step_rows if resident else 0

    @pl.when(step == 0)
    def _():
        for copy in copies:
            copy.start()
        total[...] = jnp.zeros_like(total)
        mix_wide[...] = jnp.zeros_like(mix_wide)

    @pl.when(step < front)
    def _():
        h = part_ref[0]
        levels = lax.broadcasted_iota(jnp.int32, (bins, cols), 0)
        for g in range(step_groups):
            group = []
            for r in range(GROUP):
                i = g * GROUP + r
                own = own_ref[base + i].astype(F32)
                halves = []
                for u in range(parts):
                    half = received[0][base + i]
                    for shift in range(1, parts):
                        half = jnp.where(
                            lax.rem(h + parts - u, parts) == shift, received[shift][base + i], half
                        )
                    halves.append(half)
                symmetric = own + jnp.concatenate(halves, axis=1).astype(F32)
                top = jnp.max(symmetric, axis=0, keepdims=True)
                raised = jnp.exp(symmetric - top)
                scale = 2.0 / jnp.sum(raised, axis=0, keepdims=True)
                hit = jnp.where(levels == target_ref[i : i + 1, :], 2.0, 0.0)
                group.append((raised * scale - hit).astype(BF16))
            slope = jnp.concatenate(group, axis=0).T
            slopes[step * step_groups + g] = slope
            out = contract(slope, weight_wide_ref[...], 1, 0).astype(BF16)
            for r in range(GROUP):
                grad_ref[g * GROUP + r] = out[:, r * width : (r + 1) * width]

    @pl.when(step == front)
    def _():
        for copy in copies:
            copy.wait()
        half_groups = max(1, groups // 2)

        def add_tile(t, carry):
            for x in range(tile):
                for r in range(GROUP):
                    rows = pl.ds((x * GROUP + r) * bins, bins)
                    at = r * features
                    mix_wide[rows, at : at + features] = (
                        mix[t * tile + x, :, at % 128 : at % 128 + features]
                    )
            factor = factors[pl.ds(pl.multiple_of(t * tile * seqs, tile * seqs), tile * seqs), :]
            for g in range(groups):
                spread = contract(factor, slopes[g], 1, 0).astype(BF16)
                for x in range(tile):
                    mixed[g * seqs : (g + 1) * seqs, x * GROUP * bins : (x + 1) * GROUP * bins] = (
                        spread[x * seqs : (x + 1) * seqs, :]
                    )
            for g in range(0, groups, half_groups):
                rows = slice(g * seqs, (g + half_groups) * seqs)
                term = contract(mixed[rows, :], mix_wide[...], 1, 0)
                for c in range(total.shape[0]):
                    total[c, rows, :] += term[:, c * 128 : (c + 1) * 128]
            return carry

        lax.fori_loop(0, xs // tile, add_tile, 0)
        slot_seqs = seqs // slots
        for s in range(seqs):
            slot, rest = divmod(s, slot_seqs)
            device, k = divmod(rest, device_seqs)
            other, pair = divmod(slot, slots // parts)
            block = part_ref[1] ^ pair
            device += (block * parts + lax.rem(part_ref[0] + other, parts)) * (devices // slots)
            for c in range(total.shape[0]):
                norm_ref[device, k * groups : (k + 1) * groups, c * 128 : (c + 1) * 128] = (
                    total[c, pl.ds(s, groups, stride=seqs), :].astype(BF16)
                )


def pair_step(
    part, shape, own, received, targets, weight_wide, factors, mix, grad,
    first_row, seqs, devices, slots, ahead, resident,
):
    _, cols, width = shape
    bins = own.shape[1]
    features = mix.shape[2] // 2
    parts = len(received)
    chunk_rows = received[0].shape[0]
    step_rows = min(16, chunk_rows)
    groups = chunk_rows // GROUP
    xs = factors.shape[0] // seqs
    tile = max(1, min(16, 1024 // seqs))
    front = chunk_rows // step_rows
    near = lambda s: jnp.minimum(s, front - 1)
    anywhere = pl.BlockSpec(memory_space=pl.ANY)
    if resident:
        mine = held = moved = pl.BlockSpec(memory_space=pltpu.VMEM)
    else:
        held = pl.BlockSpec((step_rows, bins, cols // parts), lambda s, p: (near(s), 0, 0))
        mine = pl.BlockSpec((step_rows, bins, cols), lambda s, p: (near(s), 0, 0))
        moved = anywhere
    there = lambda s: first_row // step_rows + jnp.minimum(s, front - 1)
    const2 = lambda s, p: (0, 0)
    norm_shape = (devices, seqs // devices * groups, GROUP * features)
    return pl.pallas_call(
        functools.partial(pair_kernel, parts, slots, front, tile, resident),
        grid_spec=pltpu.PrefetchScalarGridSpec(
            num_scalar_prefetch=1,
            grid=(front + 1,),
            in_specs=[mine]
            + [held] * parts
            + [
                pl.BlockSpec((step_rows, cols), lambda s, p: (there(s), 0)),
                pl.BlockSpec((GROUP * bins, GROUP * width), const2),
            ]
            + [moved] * 2
            + [pl.BlockSpec(memory_space=pltpu.HBM)] * len(grad)
            + [anywhere] * len(ahead),
            out_specs=[
                pl.BlockSpec((step_rows, cols, width), lambda s, p: (there(s), 0, 0)),
                pl.BlockSpec(norm_shape, lambda s, p: (0, 0, 0)),
            ],
            scratch_shapes=[
                pltpu.VMEM((groups, cols, GROUP * bins), BF16),
                pltpu.VMEM((tile * GROUP * bins, GROUP * features), BF16),
                pltpu.VMEM((groups * seqs, tile * GROUP * bins), BF16),
                pltpu.VMEM((GROUP * features // 128, groups * seqs, 128), F32),
            ]
            + ([] if resident else [
                pltpu.VMEM(factors.shape, BF16),
                pltpu.VMEM(mix.shape, BF16),
                pltpu.SemaphoreType.DMA((2,)),
            ]),
        ),
        out_shape=[
            jax.ShapeDtypeStruct(shape, BF16),
            jax.ShapeDtypeStruct(norm_shape, BF16),
        ],
        input_output_aliases={parts + 6: 0} if grad else {},
        compiler_params=pltpu.CompilerParams(vmem_limit_bytes=LEAN_BYTES if resident else VMEM_BYTES),
        cost_estimate=LONG,
        name="pair_step",
    )(part, own, *received, targets, weight_wide, factors, mix, *grad, *ahead)


def norm_forward(features):
    centered = features - jnp.mean(features, axis=0, keepdims=True)
    scale_inv = lax.rsqrt(jnp.mean(centered * centered, axis=0, keepdims=True) + 1e-05)
    return centered * scale_inv, scale_inv


def norm_backward(incoming, normed, scale_inv):
    first_mean = jnp.mean(incoming, axis=0, keepdims=True)
    second_mean = jnp.mean(incoming * normed, axis=0, keepdims=True)
    return scale_inv * (incoming - first_mean - normed * second_mean)


def transition_kernel(
    pieces, rows, col_devices, entry_ref, arriving_ref, mean_gain_ref, gain_ref, gate_up_t_ref,
    gate_up_ref, down_ref, down_t_ref, *refs,
):
    arrived, (out_ref, incoming) = refs[:-2], refs[-2:]
    hidden = down_ref.shape[0]
    seqs, features, positions = out_ref.shape
    groups = rows // GROUP
    row = lax.broadcasted_iota(jnp.int32, (groups, rows), 0)
    col = lax.broadcasted_iota(jnp.int32, (groups, rows), 1)
    spread = [jnp.where(col == GROUP * row + r, 1.0, 0.0).astype(BF16) for r in range(GROUP)]

    for s in range(seqs):
        for block in range(positions // rows):
            sums = []
            for which, at, count in pieces:
                at += s * count
                sums.append(
                    sum(
                        arrived[which][block * col_devices + c, at : at + count, :].astype(F32)
                        for c in range(col_devices)
                    )
                )
            field = jnp.concatenate(sums, axis=0).astype(BF16)
            incoming[s, :, block * rows : (block + 1) * rows] = sum(
                contract(field[:, r * features : (r + 1) * features], spread[r], 0, 0)
                for r in range(GROUP)
            )

    gain = gain_ref[...]
    for s in range(seqs):
        entry = entry_ref[s].astype(F32)
        normed, scale_inv = norm_forward(entry)
        normed_input = (normed * gain).astype(BF16)
        both = contract(gate_up_t_ref[...], normed_input, 1, 0)
        gate, up = both[:hidden], both[hidden:]
        sig = jax.nn.sigmoid(gate)
        silu = gate * sig
        msa_out = entry + contract(down_t_ref[...], (silu * up).astype(BF16), 1, 0)
        second_normed, second_scale = norm_forward(msa_out)
        middle = arriving_ref[s].astype(F32) + norm_backward(
            incoming[s] * mean_gain_ref[...], second_normed, second_scale
        )
        hidden_grad = contract(down_ref[...], middle.astype(BF16), 1, 0)
        gate_grad = (hidden_grad * up * sig * (1.0 + gate * (1.0 - sig))).astype(BF16)
        up_grad = (hidden_grad * silu).astype(BF16)
        normed_grad = contract(
            gate_up_ref[...], jnp.concatenate([gate_grad, up_grad], axis=0), 1, 0
        )
        out = middle + norm_backward(normed_grad * gain, normed, scale_inv)
        out_ref[s] = out.astype(BF16)


def transition(
    entry, arriving, arrived, pieces, rows, col_devices, mean_gain, gain, gate_weight, up_weight,
    down_weight,
):
    features = entry.shape[1]
    gate_up = jnp.concatenate([gate_weight, up_weight], axis=1)
    return pl.pallas_call(
        functools.partial(transition_kernel, pieces, rows, col_devices),
        out_shape=jax.ShapeDtypeStruct(entry.shape, BF16),
        scratch_shapes=[pltpu.VMEM(entry.shape, F32)],
        compiler_params=pltpu.CompilerParams(vmem_limit_bytes=VMEM_BYTES),
        name="transition",
    )(entry, arriving, mean_gain[:, None], gain[:, None], gate_up.T, gate_up, down_weight,
      down_weight.T, *arrived)


def chunk_plan(rows):
    size = max(16, rows // 4)
    return [(at, min(size, rows - at)) for at in range(0, rows, size)]


def per_device(
    pair_activation,
    target_distance_bins,
    distogram_weight,
    distogram_bias,
    outer_pair_weight,
    stored_lhs_operand,
    stored_rhs_operand,
    left_projection_weight,
    right_projection_weight,
    outer_mean_norm_gain,
    transition_norm_gain,
    gate_weight,
    up_weight,
    down_weight,
    side_stack_entry,
    arriving_stack_derivative,
):
    rows, cols, _ = pair_activation.shape
    width, bins = distogram_weight.shape
    factor_width = stored_lhs_operand.shape[1]
    features = left_projection_weight.shape[0]
    row_devices = lax.axis_size("row")
    col_devices = lax.axis_size("col")
    parts = row_devices // col_devices
    seqs = stored_lhs_operand.shape[0] * row_devices
    row_index = lax.axis_index("row").astype(jnp.int32)
    part = jnp.stack([row_index % parts, row_index // parts])
    weight_t = distogram_weight.T
    bias = distogram_bias[None, :]
    same = jnp.eye(GROUP, dtype=BF16)
    weight_wide = (same[:, None, :, None] * weight_t[None, :, None, :]).reshape(
        GROUP * bins, GROUP * width
    )

    blocks = row_devices // parts
    own = join([stored_rhs_operand, stored_lhs_operand], 1)
    others = []
    for flip in range(1, blocks):
        pairs = [((n ^ flip) * parts + h, n * parts + h) for n in range(blocks) for h in range(parts)]
        others.append(lax.ppermute(own, "row", pairs))

    across = join([own] + others, 0)
    shifted = [across]
    for shift in range(1, parts):
        pairs = [
            (n * parts + (h + shift) % parts, n * parts + h)
            for n in range(blocks) for h in range(parts)
        ]
        shifted.append(lax.ppermute(across, "row", pairs))
    factors = jnp.concatenate(shifted).reshape(seqs, 2 * factor_width, cols)
    factors = factors.swapaxes(0, 1).reshape(2 * factor_width * seqs, cols)

    outer_weight = outer_pair_weight.astype(F32).reshape(factor_width, factor_width, width)
    by_bin = jnp.einsum(
        "pb,cep->bce", distogram_weight.astype(F32), outer_weight, precision=lax.Precision.HIGHEST
    )
    mix_right = jnp.einsum(
        "mc,bce->ebm", left_projection_weight.astype(F32), by_bin, precision=lax.Precision.HIGHEST
    )
    mix_left = jnp.einsum(
        "me,bce->cbm", right_projection_weight.astype(F32), by_bin, precision=lax.Precision.HIGHEST
    )
    mix = (jnp.concatenate([mix_right, mix_left], axis=0) / seqs).astype(BF16)
    mix = jnp.concatenate([mix, mix], axis=2)

    devices = row_devices * col_devices
    exchange = functools.partial(
        lax.all_to_all, axis_name=AXES, split_axis=0, concat_axis=0, tiled=True
    )
    chunks = chunk_plan(rows)
    count = len(chunks)
    leg_pairs = first_leg(col_devices, parts)
    first, logits, sent, relayed, received = [], [], [], [], []
    owns, norm_parts, arrived, grad = [], [], [], []
    for n in range(count + 2):
        while len(first) < min(2, count):
            first.append(
                mirror_logits(
                    part, pair_activation, weight_t, bias, *chunks[len(first)], parts, first[-1:]
                )
            )
        for m in range(len(logits), min(count, n + 2)):
            before = others if m < 2 else relayed[m - 2] + sum(received[: m - 2][-1:], [])
            logits.append(tie(first[m], before))
            sent.append(lax.ppermute(logits[m], AXES, leg_pairs))
        while len(first) < count:
            first.append(
                mirror_logits(
                    part, pair_activation, weight_t, bias, *chunks[len(first)], parts,
                    logits[-1:] if len(first) == 2 else first[-1:],
                )
            )
        if n >= min(2, count):
            now = n - min(2, count)
            if now < count:
                ahead = logits[n : n + 1] + [x for arrays in relayed[now + 1 :] for x in arrays]
                if now == count - 1 and now > 0:
                    early = join(norm_parts, 1, received[now])
                    arrived.append(exchange(early))
                    ahead = [early]
                *grad, norm_part = pair_step(
                    part, pair_activation.shape, owns[now], received[now], target_distance_bins,
                    weight_wide, factors, mix, grad, chunks[now][0], seqs, devices, row_devices,
                    ahead, now < count - 1,
                )
                norm_parts.append(norm_part)
        if n < count:
            before = [[across, mix, weight_wide], [factors]][n] if n < 2 else [norm_parts[n - 2]]
            if n == 0:
                before = before + first[2:]
            if n < 2:
                for chunk in chunks[2 * n :][: 2 if n == 0 else count]:
                    owns.append(
                        own_logits(
                            pair_activation, weight_t, bias, *chunk,
                            owns[-1:] + (first[-1:] if n == 0 else relayed[0]),
                        )
                    )
                before = before + owns[2 * n :]
            relayed.append(list(split(sent[n], before)))
            received.append(
                [
                    lax.ppermute(piece, AXES, second_leg(col_devices, parts, shift))
                    for shift, piece in enumerate(relayed[n])
                ]
            )
    final = norm_parts[-1]
    if arrived:
        final, arrived[0] = lax.optimization_barrier((final, arrived[0]))
    arrived.append(exchange(final))
    pieces = []
    for n, part_sums in enumerate(norm_parts):
        last = n == len(chunks) - 1 and n > 0
        at = 0 if last else sum(x.shape[1] for x in norm_parts[:n])
        pieces.append((int(last), at, chunks[n][1] // GROUP))
    alignment_gradient = transition(
        side_stack_entry, arriving_stack_derivative, arrived, pieces, rows, col_devices,
        outer_mean_norm_gain, transition_norm_gain, gate_weight, up_weight, down_weight,
    )
    return grad[0], alignment_gradient


def solution(mesh):
    return jax.shard_map(
        per_device,
        mesh=mesh,
        in_specs=(
            P("row", "col", None),
            P("row", "col"),
            P(),
            P(),
            P(),
            P("row", None, "col"),
            P("row", None, "col"),
            P(),
            P(),
            P(),
            P(),
            P(),
            P(),
            P(),
            P(AXES, None, None),
            P(AXES, None, None),
        ),
        out_specs=(P("row", "col", None), P(AXES, None, None)),
        check_vma=False,
    )
```
